256 devices in a mesh: dp: 64 (over y, z, x_hi), mp: 4 (over x_lo, core).
Axes of the slice: x: 4 (x_hi: 2, x_lo: 2; x = x_hi * 2 + x_lo), y: 4, z: 8, core: 2. Of those that a mesh axis runs over, the one named last changes fastest.
Arguments:
- queries: bfloat16 [8192, 8192], P('dp', 'mp'), may hold values from -8 to 8
- response_keys: bfloat16 [8192, 1024], P('dp', 'mp'), may hold values from -6 to 6
- response_values: bfloat16 [8192, 1024], P('dp', 'mp'), may hold values from -6 to 6
- prompt_keys: bfloat16 [4096, 1024], P('dp', 'mp'), may hold values from -6 to 6
- prompt_value_rows: bfloat16 [4096, 1024], P('dp', 'mp'), may hold values from -6 to 6
- readout: bfloat16 [8192, 8192], P('dp', 'mp'), may hold values from -0.1875 to 0.1875
- prox_logp: float32 [8192], P('dp'), may hold values from -1.75 to 1.75
- behave_logp: float32 [8192], P('dp'), may hold values from -1.75 to 1.75
- advantage: float32 [64], P('dp'), may hold values from -6 to 6
- lengths: int32 [64], P('dp'), may hold values from 1 to 128, 4096 in all
- loss_mask: int32 [8192], P('dp'), may hold values 0 or 1
Outputs:
- grad_queries: bfloat16 [8192, 8192], P('dp', 'mp')
- response_key_gradient: bfloat16 [8192, 1024], P('dp', 'mp')
- response_value_gradient: bfloat16 [8192, 1024], P('dp', 'mp')
- prompt_key_gradient: bfloat16 [4096, 1024], P('dp', 'mp')
- prompt_value_gradient: bfloat16 [4096, 1024], P('dp', 'mp')
- response_loss_terms: float32 [64], P('dp')
The draws below stay inside these ranges and needn't reach their ends.
Inputs may be any that keep to these rules, and one draw needn't show every extreme that they name: Response j holds real tokens in slots t < lengths[j]; some response has all 128.
All inputs are finite; a program needn't handle non-finite values. No bound on the sum of `lengths` or of `loss_mask` on one device may be relied on, other than what follows from the above.
Results may differ from the reference program's by a relative error of at most 0.012.
The reference program's roundings to bfloat16 on the way (of `probs_half`, `grad_out` and `grad_scores`) count: a program that leaves them out, or rounds other values in their place, can miss the bound.
Values may be sent and summed in bfloat16 or wider, within the bound.
A program may use at most 64 MiB of HBM per device.

```python
import math
import jax
import jax.numpy as jnp
import numpy as np
from jax import lax

QUERY_HEADS = 64
KEY_VALUE_HEADS = 8
HEAD_SIZE = 128
PROMPT_TOKENS = 1024
RESPONSE_SLOTS = 128
STRETCH = 16
PROMPTS = 4
PTOK_DEV = 64
TOKEN_SLOTS = 8192
PROMPT_ROW_TOTAL = 4096
N_DP = 64


def draw_queries(key, part):
    key = jax.random.fold_in(key, 11)
    value_offset = jnp.clip(jax.random.normal(key, (TOKEN_SLOTS, QUERY_HEADS * HEAD_SIZE), jnp.float32), -6.0, 6.0)
    return value_offset.astype(jnp.bfloat16)


def draw_prompt_keys(key, part):
    key = jax.random.fold_in(key, 12)
    value_offset = jnp.clip(jax.random.normal(key, (PROMPT_ROW_TOTAL, KEY_VALUE_HEADS * HEAD_SIZE), jnp.float32), -6.0, 6.0)
    return value_offset.astype(jnp.bfloat16)


def touch_ends(values, key, low, top_value):
    longest = values.shape.index(max(values.shape))
    spots = []
    for shift in (0, 1):
        where = [jax.random.randint(jax.random.fold_in(key, axis), (), 0, length) for axis, length in enumerate(values.shape)]
        where[longest] = (where[longest] + shift) % values.shape[longest]
        spots.append(tuple(where))
    return values.at[spots[0]].set(low).at[spots[1]].set(top_value)


def block_levels(stream_key, shape, split, smallest, top_value):
    gain, own = 1.0, jax.random.fold_in(stream_key, 6)
    for dim, parts in split:
        draws = jnp.exp(jax.random.uniform(jax.random.fold_in(own, dim), (parts,), jnp.float32, smallest / len(split), top_value / len(split)))
        gain = gain * jnp.repeat(draws, shape[dim] // parts).reshape([-1 if axis == dim else 1 for axis in range(len(shape))])
    return gain


def profile(count, total, limit, skew):
    portions = [(1 << 20) // math.isqrt(standing ** skew) + 1 for standing in range(2, count + 1)]
    surplus, given = total - limit - (count - 1), [1] * (count - 1)
    while surplus > 0:
        movable = [i for i in range(count - 1) if given[i] < limit]
        whole, remaining = sum([portions[i] for i in movable]), surplus
        for i in movable:
            addition = min(limit - given[i], max(1, remaining * portions[i] // whole), surplus)
            given[i] = given[i] + addition
            surplus = surplus - addition
    return np.array([limit] + given)


def uneven(own_key, number_of, total, reach, skew):
    if number_of == 2:
        one = jax.random.randint(own_key, (), max(1, total - reach), min(reach, total - 1) + 1)
        return jnp.stack([one, total - one])
    sizes = jnp.asarray(profile(number_of, total, reach, skew), jnp.int32)
    couples = (number_of - 1) // 2
    source_of, receiver = sizes[1:1 + 2 * couples:2], sizes[2:2 + 2 * couples:2]
    room = jnp.minimum(source_of - 1, reach - receiver)
    passed = jax.random.randint(jax.random.fold_in(own_key, 1), (couples,), 0, 1 << 20) % (room + 1)
    sizes = sizes.at[1:1 + 2 * couples:2].set(source_of - passed).at[2:2 + 2 * couples:2].set(receiver + passed)
    return sizes[jax.random.permutation(jax.random.fold_in(own_key, 2), number_of)]


def normal_values(stream_key, shape, scale, reach, cuts=(), held_as=jnp.bfloat16):
    array = jax.random.normal(stream_key, shape, jnp.float32) * scale
    if len(cuts) > 0:
        array = block_levels(stream_key, shape, cuts, -0.22, 0.18) * array
    return jnp.clip(array, min=-reach, max=reach).astype(held_as)


def setup_inputs(seed: int = 0) -> dict:
    keys = jax.random.split(jax.random.key(seed), 12)
    queries = draw_queries(jax.random.fold_in(keys[11], 71), 0)
    response_keys = normal_values(keys[1], (TOKEN_SLOTS, KEY_VALUE_HEADS * HEAD_SIZE), 1.0, 6.0, ((0, 64), (1, 4)))
    response_values = normal_values(keys[2], (TOKEN_SLOTS, KEY_VALUE_HEADS * HEAD_SIZE), 1.0, 6.0, ((0, 64), (1, 4)))
    prompt_keys = draw_prompt_keys(jax.random.fold_in(keys[11], 71), 0)
    prompt_value_rows = normal_values(keys[4], (PROMPT_ROW_TOTAL, KEY_VALUE_HEADS * HEAD_SIZE), 1.0, 6.0, ((0, 64), (1, 4)))
    readout = normal_values(keys[5], (TOKEN_SLOTS, QUERY_HEADS * HEAD_SIZE), 0.03, 0.1875, ((0, 64), (1, 4)))
    prox_logp = normal_values(keys[6], (TOKEN_SLOTS,), 0.3, 1.75, ((0, 64),), jnp.float32)
    behave_logp = normal_values(keys[7], (TOKEN_SLOTS,), 0.3, 1.75, ((0, 64),), jnp.float32)
    advantage = normal_values(keys[8], (N_DP,), 1.0, 6.0, ((0, 64),), jnp.float32)
    lengths = uneven(keys[9], N_DP, N_DP * RESPONSE_SLOTS // 2, RESPONSE_SLOTS, 1).astype(jnp.int32)
    loss_mask = touch_ends((jax.random.randint(keys[10], (TOKEN_SLOTS,), 0, 8) < 7).astype(jnp.int32), jax.random.fold_in(keys[10], 1), 0, 1)
    return dict(queries=queries, response_keys=response_keys, response_values=response_values, prompt_keys=prompt_keys, prompt_value_rows=prompt_value_rows, readout=readout, prox_logp=prox_logp, behave_logp=behave_logp, advantage=advantage, lengths=lengths, loss_mask=loss_mask)


clip_width = 0.2

def rounded(value):
    return lax.optimization_barrier(value.astype(jnp.bfloat16)).astype(jnp.float32)

def allowed_mask(query_rows, prompt_len):
    key_ids = lax.broadcasted_iota(jnp.int32, (query_rows, prompt_len + query_rows), 1)
    query_ids = lax.broadcasted_iota(jnp.int32, (query_rows, prompt_len + query_rows), 0)
    return (key_ids < prompt_len) | (key_ids - prompt_len <= query_ids)

def policy_terms(log_prob, prox_part, behave_part, adv_value, valid, length_value, row_count):
    prob_ratio = jnp.exp(log_prob - prox_part)
    importance = jnp.exp(prox_part - behave_part)
    squashed = jnp.tanh((prob_ratio - 1.0) / clip_width)
    clipped = 1.0 + clip_width * squashed
    token_scale = jnp.where(valid, row_count / length_value, 0.0)
    objective = jnp.minimum(prob_ratio * adv_value, clipped * adv_value)
    response_loss_terms = -jnp.sum(token_scale * importance * objective)
    clip_slope = jnp.where(adv_value * (prob_ratio - 1.0) > 0, 1.0 - squashed * squashed, 1.0)
    grad_logprob = -token_scale * importance * adv_value * prob_ratio * clip_slope
    return (response_loss_terms, grad_logprob)

def reference(queries, response_keys, response_values, prompt_keys, prompt_value_rows, readout, prox_logp, behave_logp, advantage, lengths, loss_mask):
    head_groups = QUERY_HEADS // KEY_VALUE_HEADS
    score_scale = 1.0 / math.sqrt(HEAD_SIZE)
    allowed = allowed_mask(RESPONSE_SLOTS, PROMPT_TOKENS)
    row_ids = jnp.arange(RESPONSE_SLOTS, dtype=jnp.int32)
    kv_width = KEY_VALUE_HEADS * HEAD_SIZE
    key_blocks = prompt_keys.reshape(STRETCH, PROMPTS, PTOK_DEV, kv_width)
    value_blocks = prompt_value_rows.reshape(STRETCH, PROMPTS, PTOK_DEV, kv_width)

    def one_response(running, response):
        key_total, value_total = running
        first_row = (response * RESPONSE_SLOTS).astype(jnp.int32)
        prompt_id = (response % PROMPTS).astype(jnp.int32)
        query_tile = lax.dynamic_slice_in_dim(queries, first_row, RESPONSE_SLOTS, 0).reshape(RESPONSE_SLOTS, KEY_VALUE_HEADS, head_groups, HEAD_SIZE).astype(jnp.float32)
        loaded_block = lax.dynamic_slice_in_dim(readout, first_row, RESPONSE_SLOTS, 0).reshape(RESPONSE_SLOTS, KEY_VALUE_HEADS, head_groups, HEAD_SIZE).astype(jnp.float32)
        prompt_key_rows = lax.dynamic_index_in_dim(key_blocks, prompt_id, 1, keepdims=False).reshape(PROMPT_TOKENS, kv_width)
        prompt_val_rows = lax.dynamic_index_in_dim(value_blocks, prompt_id, 1, keepdims=False).reshape(PROMPT_TOKENS, kv_width)
        every_key = jnp.concatenate([prompt_key_rows, lax.dynamic_slice_in_dim(response_keys, first_row, RESPONSE_SLOTS, 0)], 0)
        every_key = every_key.reshape(PROMPT_TOKENS + RESPONSE_SLOTS, KEY_VALUE_HEADS, HEAD_SIZE).astype(jnp.float32)
        every_value = jnp.concatenate([prompt_val_rows, lax.dynamic_slice_in_dim(response_values, first_row, RESPONSE_SLOTS, 0)], 0)
        every_value = every_value.reshape(PROMPT_TOKENS + RESPONSE_SLOTS, KEY_VALUE_HEADS, HEAD_SIZE).astype(jnp.float32)
        scores = jnp.einsum('rkgd,nkd->kgrn', query_tile, every_key) * score_scale
        scores = jnp.where(allowed, scores, -jnp.inf)
        maxima = lax.optimization_barrier(jnp.max(scores, axis=-1, keepdims=True))
        log_total = maxima + jnp.log(lax.optimization_barrier(jnp.sum(jnp.exp(scores - maxima), axis=-1, keepdims=True)))
        soft_probs = jnp.exp(scores - log_total)
        probs_half = rounded(soft_probs)
        attended = jnp.einsum('kgrn,nkd->rkgd', probs_half, every_value)
        head_dot = lax.optimization_barrier(jnp.sum(loaded_block * attended, axis=-1))
        log_prob = lax.optimization_barrier(jnp.sum(head_dot, axis=(1, 2)))
        mask_part = lax.dynamic_slice_in_dim(loss_mask, first_row, RESPONSE_SLOTS, 0)
        length_value = lengths[response]
        valid = (row_ids < length_value) & (mask_part == 1)
        prox_part = lax.dynamic_slice_in_dim(prox_logp, first_row, RESPONSE_SLOTS, 0)
        behave_part = lax.dynamic_slice_in_dim(behave_logp, first_row, RESPONSE_SLOTS, 0)
        response_loss_terms, grad_logprob = policy_terms(log_prob, prox_part, behave_part, advantage[response], valid, length_value.astype(jnp.float32), RESPONSE_SLOTS)
        grad_out = rounded(grad_logprob[:, None, None, None] * loaded_block)
        row_delta = grad_logprob[:, None, None] * head_dot
        grad_probs = jnp.einsum('rkgd,nkd->kgrn', grad_out, every_value)
        grad_scores = rounded(soft_probs * (grad_probs - jnp.transpose(row_delta, (1, 2, 0))[..., None]))
        query_gradient = (jnp.einsum('kgrn,nkd->rkgd', grad_scores, every_key) * score_scale).astype(jnp.bfloat16)
        key_gradient = jnp.einsum('kgrn,rkgd->nkd', grad_scores, query_tile) * score_scale
        value_gradient = jnp.einsum('kgrn,rkgd->nkd', probs_half, grad_out)
        key_total = lax.dynamic_update_index_in_dim(key_total, lax.dynamic_index_in_dim(key_total, prompt_id, 0, keepdims=False) + key_gradient[:PROMPT_TOKENS], prompt_id, 0)
        value_total = lax.dynamic_update_index_in_dim(value_total, lax.dynamic_index_in_dim(value_total, prompt_id, 0, keepdims=False) + value_gradient[:PROMPT_TOKENS], prompt_id, 0)
        output_rows = (query_gradient.reshape(RESPONSE_SLOTS, QUERY_HEADS * HEAD_SIZE), key_gradient[PROMPT_TOKENS:].reshape(RESPONSE_SLOTS, kv_width).astype(jnp.bfloat16), value_gradient[PROMPT_TOKENS:].reshape(RESPONSE_SLOTS, kv_width).astype(jnp.bfloat16), response_loss_terms)
        return ((key_total, value_total), output_rows)
    initial_totals = (jnp.zeros((PROMPTS, PROMPT_TOKENS, KEY_VALUE_HEADS, HEAD_SIZE), jnp.float32), jnp.zeros((PROMPTS, PROMPT_TOKENS, KEY_VALUE_HEADS, HEAD_SIZE), jnp.float32))
    running_totals, piled_rows = lax.scan(one_response, initial_totals, jnp.arange(N_DP, dtype=jnp.int32))

    def laid_out(total):
        blocks = total.reshape(PROMPTS, STRETCH, PTOK_DEV, kv_width)
        return jnp.transpose(blocks, (1, 0, 2, 3)).reshape(PROMPT_ROW_TOTAL, kv_width).astype(jnp.bfloat16)
    grad_queries = piled_rows[0].reshape(TOKEN_SLOTS, QUERY_HEADS * HEAD_SIZE)
    response_key_gradient = piled_rows[1].reshape(TOKEN_SLOTS, kv_width)
    response_value_gradient = piled_rows[2].reshape(TOKEN_SLOTS, kv_width)
    return (grad_queries, response_key_gradient, response_value_gradient, laid_out(running_totals[0]), laid_out(running_totals[1]), piled_rows[3])
```

```python
import functools
import math

import jax
import jax.numpy as jnp
from jax import lax
from jax.experimental import pallas as pl
from jax.experimental.pallas import tpu as pltpu
from jax.sharding import PartitionSpec as P

D = 128
HK = 2
NJ = 4
JR = 256
CK = 256
BK = 64
SCALE = 1.0 / math.sqrt(D)
C1 = SCALE * math.log2(math.e)
CLIP = 0.2
MESH = pl.DeviceIdType.MESH
F32 = jnp.float32
BF16 = jnp.bfloat16

OWN, UP, DOWN, FAR = 0, 1, 2, 3
RESP = 4 * CK
KEYS = RESP + 128
CHUNKS = [(0, CK), (CK, CK), (2 * CK, CK), (3 * CK, CK), (RESP, 128)]


def dot_t(a, b):
    return lax.dot_general(a, b, (((1,), (1,)), ((), ())), preferred_element_type=F32)


def dot_n(a, b):
    return jnp.dot(a, b, preferred_element_type=F32)


def kernel(
    q_hbm, rk_hbm, rv_hbm, pk_hbm, pv_hbm, ro_hbm, prox_hbm, beh_hbm, adv_hbm, len_hbm, mask_hbm,
    gq_hbm, grk_hbm, grv_hbm, gpk_hbm, gpv_hbm, loss_hbm,
    kv, kvt, qs, rs, rst, es, pb, ds, ms, ls, fs, hds, do,
    lpx, tok, tokm, adv_s, len_s, loss_s,
    y2s, y2r, y1s, y1r, joins, zs, zr, ownz,
    gq_v, gr_v, gp_v,
    ld_sem, out_sem,
    gz_s, gz_r, gy_s, gy_r, lp_s, lp_r, y2_s, y2_rs, y1_s, y1_rs, z_s, z_rs,
):
    dp = lax.axis_index("dp")
    mp = lax.axis_index("mp")
    pc = lax.axis_size("dp") // 16
    mpn = lax.axis_size("mp")
    s = lax.rem(dp, pc)
    gp = dp // pc
    y = gp // 4
    z = lax.rem(gp, 4)

    def peer(dy, dz):
        yy = lax.rem(y + dy + 4, 4)
        zz = lax.rem(z + dz + 4, 4)
        return (((yy * 4 + zz) * pc + s), mp)

    y_up, y_dn = peer(1, 0), peer(-1, 0)
    z_up, z_dn, z_far = peer(0, 1), peer(0, -1), peer(0, 2)
    mates = [(dp, lax.rem(mp + k, mpn)) for k in range(1, mpn)]

    barrier = pltpu.get_barrier_semaphore()
    friends = [y_up, y_dn, z_up, z_dn] + mates
    for f in friends:
        pl.semaphore_signal(barrier, inc=1, device_id=f, device_id_type=MESH)

    own_loads = []
    for t, src in enumerate((pk_hbm, pv_hbm)):
        for h in range(HK):
            c = pltpu.make_async_copy(
                src.at[:, h * D:(h + 1) * D], kv.at[t, h, 0:BK, :], ld_sem.at[t * HK + h]
            )
            c.start()
            own_loads.append(c)
    resp_loads = []
    for t, src in enumerate((rk_hbm, rv_hbm)):
        for h in range(HK):
            c = pltpu.make_async_copy(
                src.at[:, h * D:(h + 1) * D], kv.at[t, h, RESP:KEYS, :], ld_sem.at[4 + t * HK + h]
            )
            c.start()
            resp_loads.append(c)
    for h in range(HK):
        for t, (src, dst) in enumerate(((q_hbm, qs), (ro_hbm, rs))):
            for i in range(8):
                n = h * 8 + i
                pltpu.make_async_copy(
                    src.at[:, n * D:(n + 1) * D],
                    dst.at[h, i // 2, (i % 2) * 128:(i % 2 + 1) * 128, :],
                    ld_sem.at[8 + t * HK + h],
                ).start()
    small = [
        pltpu.make_async_copy(prox_hbm, tok.at[0], ld_sem.at[12]),
        pltpu.make_async_copy(beh_hbm, tok.at[1], ld_sem.at[13]),
        pltpu.make_async_copy(mask_hbm, tokm, ld_sem.at[14]),
        pltpu.make_async_copy(adv_hbm, adv_s, ld_sem.at[15]),
        pltpu.make_async_copy(len_hbm, len_s, ld_sem.at[16]),
    ]
    for c in small:
        c.start()

    def wait_rows(h):
        for t, dst in enumerate((qs, rs)):
            pltpu.make_async_copy(dst.at[h], dst.at[h], ld_sem.at[8 + t * HK + h]).wait()

    def turn_rows(h):
        for j in range(NJ):
            rst[h, j] = rs[h, j].T

    sends = []

    def send(src, dst, ss, rsem, to):
        c = pltpu.make_async_remote_copy(
            src_ref=src, dst_ref=dst, send_sem=ss, recv_sem=rsem, device_id=to, device_id_type=MESH
        )
        c.start()
        sends.append(c)

    def arrived(dst, rsem):
        pltpu.make_async_remote_copy(
            src_ref=dst, dst_ref=dst, send_sem=rsem, recv_sem=rsem, device_id=y_up, device_id_type=MESH
        ).wait_recv()

    def kvb(t, h, dz, dy):
        lo = dz * CK + dy * BK
        tt = slice(0, 2) if t is None else slice(t, t + 1)
        return kv.at[tt, h, lo:lo + BK, :]

    def z_own():
        for t in range(2):
            for h in range(HK):
                send(kvb(1 - t, h, OWN, OWN), kvb(1 - t, h, DOWN, OWN),
                     gz_s.at[h, 1 - t, 0], gz_r.at[h, 1 - t, 0], z_up)
                send(kvb(t, h, OWN, OWN), kvb(t, h, UP, OWN),
                     gz_s.at[h, t, 1], gz_r.at[h, t, 1], z_dn)

    def z_forward(h):
        arrived(kvb(1, h, DOWN, OWN), gz_r.at[h, 1, 0])
        send(kvb(1, h, DOWN, OWN), kvb(1, h, FAR, OWN), gz_s.at[h, 1, 2], gz_r.at[h, 1, 2], z_up)
        arrived(kvb(0, h, UP, OWN), gz_r.at[h, 0, 1])
        send(kvb(0, h, UP, OWN), kvb(0, h, FAR, OWN), gz_s.at[h, 0, 2], gz_r.at[h, 0, 2], z_dn)

    def z_rest(h):
        arrived(kvb(0, h, DOWN, OWN), gz_r.at[h, 0, 0])
        arrived(kvb(1, h, UP, OWN), gz_r.at[h, 1, 1])

    def z_last(h):
        arrived(kvb(1, h, FAR, OWN), gz_r.at[h, 1, 2])
        arrived(kvb(0, h, FAR, OWN), gz_r.at[h, 0, 2])

    def y_send(h, dz):
        send(kvb(None, h, dz, OWN), kvb(None, h, dz, DOWN),
             gy_s.at[h, dz, 0], gy_r.at[h, dz, 0], y_up)
        send(kvb(None, h, dz, OWN), kvb(None, h, dz, UP),
             gy_s.at[h, dz, 1], gy_r.at[h, dz, 1], y_dn)

    def y_forward(h, dz):
        arrived(kvb(None, h, dz, DOWN), gy_r.at[h, dz, 0])
        send(kvb(1, h, dz, DOWN), kvb(1, h, dz, FAR),
             gy_s.at[h, dz, 2], gy_r.at[h, dz, 2], y_up)
        arrived(kvb(None, h, dz, UP), gy_r.at[h, dz, 1])
        send(kvb(0, h, dz, UP), kvb(0, h, dz, FAR),
             gy_s.at[h, dz, 3], gy_r.at[h, dz, 3], y_dn)

    def y_last(h, dz):
        arrived(kvb(1, h, dz, FAR), gy_r.at[h, dz, 2])
        arrived(kvb(0, h, dz, FAR), gy_r.at[h, dz, 3])

    def fwd(h, ci):
        off, nk = CHUNKS[ci]

        def body(j, _):
            sc = dot_t(kv[0, h, off:off + nk, :], qs[h, j])
            if ci == 4:
                key = lax.broadcasted_iota(jnp.int32, (nk, JR), 0)
                row = lax.broadcasted_iota(jnp.int32, (nk, JR), 1)
                sc = jnp.where(key <= lax.rem(row, 128), sc, -jnp.inf)
            m = jnp.max(sc, axis=0, keepdims=True) * C1
            e = jnp.exp2(sc * C1 - m)
            es[h, j, off:off + nk, :] = e
            ms[h, j, ci:ci + 1, :] = m
            ls[h, j, ci:ci + 1, :] = jnp.sum(e, axis=0, keepdims=True)
            return 0

        for t in range(2):
            kvt[t, h, :, off:off + nk] = kv[t, h, off:off + nk, :].T
        lax.fori_loop(0, NJ, body, 0, unroll=True)

    def normalise(h, lp):
        def body(j, lp):
            mc = ms[h, j, 0:5, :]
            m = jnp.max(mc, axis=0, keepdims=True)
            f = jnp.exp2(mc - m)
            total = jnp.sum(f * ls[h, j, 0:5, :], axis=0, keepdims=True)
            f = f / total
            fs[h, j, 0:5, :] = f
            for ci, (off, nk) in enumerate(CHUNKS):
                p = (es[h, j, off:off + nk, :] * f[ci:ci + 1, :]).astype(BF16)
                pb[h, j, off:off + nk, :] = p
            attended = dot_n(kvt[1, h], pb[h, j])
            hd = jnp.sum(attended * rst[h, j].astype(F32), axis=0, keepdims=True)
            hds[h, j, 0:1, :] = hd
            return lp + hd[:, :128] + hd[:, 128:]

        return lax.fori_loop(0, NJ, body, lp, unroll=True)

    for c in own_loads:
        c.wait()
    pl.semaphore_wait(barrier, len(friends))
    z_own()
    for h in range(HK):
        y_send(h, OWN)
    for c in resp_loads:
        c.wait()
    wait_rows(0)
    fwd(0, 4)
    for h in range(HK):
        y_forward(h, OWN)
        z_forward(h)
    for h in range(HK):
        z_rest(h)
        y_send(h, UP)
        y_send(h, DOWN)
    wait_rows(1)
    turn_rows(0)
    for h in range(HK):
        z_last(h)
        y_send(h, FAR)
    y_last(0, OWN)
    fwd(0, OWN)
    for h in range(HK):
        y_forward(h, UP)
        y_forward(h, DOWN)
    y_last(1, OWN)
    fwd(1, OWN)
    for h in range(HK):
        y_forward(h, FAR)
    fwd(1, 4)
    turn_rows(1)
    for h in range(HK):
        for dz in (UP, DOWN):
            y_last(h, dz)
            fwd(h, dz)
    lp = jnp.zeros((1, 128), F32)
    for h in range(HK):
        y_last(h, FAR)
        fwd(h, FAR)
        lp = normalise(h, lp)

    lpx[mp] = jnp.broadcast_to(lp, (8, 128))
    for k, mate in enumerate(mates):
        send(lpx.at[mp], lpx.at[mp], lp_s.at[k], lp_r.at[k], mate)
    for c in small:
        c.wait()
    for k in range(mpn - 1):
        src = lax.rem(mp + mpn - 1 - k, mpn)
        arrived(lpx.at[src], lp_r.at[k])
    log_prob = jnp.zeros((1, 128), F32)
    for k in range(mpn):
        log_prob = log_prob + lpx[k, 0:1, :]
    prox = tok[0]
    adv = adv_s[0]
    length = len_s[0]
    ratio = jnp.exp(log_prob - prox)
    importance = jnp.exp(prox - tok[1])
    squashed = jnp.tanh((ratio - 1.0) / CLIP)
    clipped = 1.0 + CLIP * squashed
    token = lax.broadcasted_iota(jnp.int32, (1, 128), 1)
    valid = (token < length) & (tokm[...] == 1)
    lens = jnp.broadcast_to(length, (1, 128)).astype(F32)
    token_scale = jnp.where(valid, 128.0 / lens, 0.0)
    objective = jnp.minimum(ratio * adv, clipped * adv)
    loss_s[0] = -jnp.sum(token_scale * importance * objective)
    slope = jnp.where(adv * (ratio - 1.0) > 0, 1.0 - squashed * squashed, 1.0)
    g = -token_scale * importance * adv * ratio * slope
    loss_out = pltpu.make_async_copy(loss_s, loss_hbm, out_sem.at[0])
    loss_out.start()
    g_rows = jnp.concatenate([g, g], axis=1)
    g_cols = jnp.broadcast_to(g, (128, 128)).T
    g_cols = jnp.concatenate([g_cols, g_cols], axis=0)

    def grad_out(h):
        def body(j, _):
            do[h, j] = (g_cols * rs[h, j].astype(F32)).astype(BF16)
            return 0

        lax.fori_loop(0, NJ, body, 0, unroll=True)

    def value_grad(h, ci):
        off, nk = CHUNKS[ci]
        acc = dot_n(pb[h, 0, off:off + nk, :], do[h, 0])
        for j in range(1, NJ):
            acc = acc + dot_n(pb[h, j, off:off + nk, :], do[h, j])
        return acc

    def key_grad(h, ci):
        off, nk = CHUNKS[ci]
        acc = None
        for j in range(NJ):
            grad_probs = dot_t(kv[1, h, off:off + nk, :], do[h, j])
            d = (es[h, j, off:off + nk, :] * fs[h, j, ci:ci + 1, :]) * (
                grad_probs - hds[h, j, 0:1, :] * g_rows
            )
            d = d.astype(BF16)
            ds[h, j, off:off + nk, :] = d
            part = dot_n(d, qs[h, j])
            acc = part if acc is None else acc + part
        return acc * SCALE

    def rows_of(dy):
        return slice(dy * BK, (dy + 1) * BK)

    def terms(dz, h):
        v = value_grad(h, dz)
        y2s[0, dz, h] = v[rows_of(FAR)].astype(BF16)
        y1s[1, 0, dz, h] = v[rows_of(DOWN)].astype(BF16)
        joins[0, dz, h] = v[rows_of(UP)]
        ownz[0, dz, h] = v[rows_of(OWN)]
        k = key_grad(h, dz)
        y2s[1, dz, h] = k[rows_of(FAR)].astype(BF16)
        y1s[0, 1, dz, h] = k[rows_of(UP)].astype(BF16)
        joins[1, dz, h] = k[rows_of(DOWN)]
        ownz[1, dz, h] = k[rows_of(OWN)]

    def y1_send(way, t, dz, h):
        send(y1s.at[way, t, dz, h], y1r.at[way, t, dz, h],
             y1_s.at[way, t, dz, h], y1_rs.at[way, t, dz, h], y_up if way == 0 else y_dn)

    def first_sends(dz, h):
        for t, to in enumerate((y_up, y_dn)):
            send(y2s.at[t, dz, h], y2r.at[t, dz, h],
                 y2_s.at[t, dz, h], y2_rs.at[t, dz, h], to)
        y1_send(0, 1, dz, h)
        y1_send(1, 0, dz, h)

    def join_sends(dz, h):
        for t in range(2):
            arrived(y2r.at[t, dz, h], y2_rs.at[t, dz, h])
            y1s[t, t, dz, h] = (joins[t, dz, h] + y2r[t, dz, h].astype(F32)).astype(BF16)
            y1_send(t, t, dz, h)

    def y_total(dz, h):
        for t in range(2):
            for way in range(2):
                arrived(y1r.at[way, t, dz, h], y1_rs.at[way, t, dz, h])
            total = ownz[t, dz, h] + (
                y1r[0, t, dz, h].astype(F32) + y1r[1, t, dz, h].astype(F32)
            )
            if dz == OWN:
                ownz[t, dz, h] = total
            else:
                zs[dz - 1, h, t] = total.astype(BF16)
        if dz != OWN:
            send(zs.at[dz - 1, h], zr.at[dz - 1, h], z_s.at[dz - 1, h], z_rs.at[dz - 1, h],
                 (z_up, z_dn, z_far)[dz - 1])

    GROUPS = ((FAR, 0), (FAR, 1), (UP, 0), (DOWN, 0), (UP, 1), (DOWN, 1), (OWN, 0), (OWN, 1))
    for h in range(HK):
        grad_out(h)
    for n, group in enumerate(GROUPS):
        terms(*group)
        first_sends(*group)
        if n >= 2:
            join_sends(*GROUPS[n - 2])
        if n >= 4:
            y_total(*GROUPS[n - 4])

    outs = []

    def put(src, dst, n):
        c = pltpu.make_async_copy(src, dst, out_sem.at[n])
        c.start()
        outs.append(c)

    for n in (6, 7):
        join_sends(*GROUPS[n])
    y_total(*GROUPS[4])
    for h in range(HK):
        gr_v[0, :, h * D:(h + 1) * D] = key_grad(h, 4).astype(BF16)
        gr_v[1, :, h * D:(h + 1) * D] = value_grad(h, 4).astype(BF16)
    put(gr_v.at[0], grk_hbm, 1)
    put(gr_v.at[1], grv_hbm, 2)

    def query_grad(h):
        def body(j, _):
            gq_v[h, j] = (dot_n(kvt[0, h], ds[h, j]) * SCALE).T.astype(BF16)
            return 0

        lax.fori_loop(0, NJ, body, 0, unroll=True)
        for i in range(8):
            n = h * 8 + i
            put(gq_v.at[h, i // 2, (i % 2) * 128:(i % 2 + 1) * 128, :],
                gq_hbm.at[:, n * D:(n + 1) * D], 5 + n)

    y_total(*GROUPS[5])
    query_grad(0)
    query_grad(1)
    for h in range(HK):
        y_total(OWN, h)
    for h in range(HK):
        for b in (2, 0, 1):
            arrived(zr.at[b, h], z_rs.at[b, h])
        for t in range(2):
            total = ownz[t, OWN, h]
            for b in range(3):
                total = total + zr[b, h, t].astype(F32)
            gp_v[t, :, h * D:(h + 1) * D] = total.astype(BF16)
    put(gp_v.at[1], gpk_hbm, 3)
    put(gp_v.at[0], gpv_hbm, 4)
    loss_out.wait()
    for c in outs:
        c.wait()
    for c in sends:
        c.wait_send()


def hand_over(*refs):
    held, sem = refs[12:18], refs[18]
    loads = [pltpu.make_async_copy(refs[n], held[n], sem.at[0, n]) for n in range(6)]
    stores = [pltpu.make_async_copy(held[n], refs[6 + n], sem.at[1, n]) for n in range(6)]
    for c in loads:
        c.start()
    for n in range(6):
        loads[n].wait()
        stores[n].start()
    for c in stores:
        c.wait()


def per_device(q, rk, rv, pk, pv, ro, prox, beh, adv, lens, mask):
    rows = q.shape[0]
    any_spec = pl.BlockSpec(memory_space=pl.ANY)
    dma = pltpu.SemaphoreType.DMA
    vm = pltpu.VMEM
    mpn = lax.axis_size("mp")
    outs = pl.pallas_call(
        kernel,
        out_shape=(
            jax.ShapeDtypeStruct(q.shape, BF16),
            jax.ShapeDtypeStruct(rk.shape, BF16),
            jax.ShapeDtypeStruct(rv.shape, BF16),
            jax.ShapeDtypeStruct(pk.shape, BF16),
            jax.ShapeDtypeStruct(pv.shape, BF16),
            jax.ShapeDtypeStruct((1,), F32),
        ),
        in_specs=[any_spec] * 11,
        out_specs=(any_spec,) * 6,
        scratch_shapes=[
            vm((2, HK, KEYS, D), BF16),
            vm((2, HK, D, KEYS), BF16),
            vm((HK, NJ, JR, D), BF16),
            vm((HK, NJ, JR, D), BF16),
            vm((HK, NJ, D, JR), BF16),
            vm((HK, NJ, KEYS, JR), F32),
            vm((HK, NJ, KEYS, JR), BF16),
            vm((HK, NJ, KEYS, JR), BF16),
            vm((HK, NJ, 8, JR), F32),
            vm((HK, NJ, 8, JR), F32),
            vm((HK, NJ, 8, JR), F32),
            vm((HK, NJ, 8, JR), F32),
            vm((HK, NJ, JR, D), BF16),
            vm((mpn, 8, 128), F32),
            vm((2, 1, 128), F32),
            vm((1, 128), jnp.int32),
            pltpu.SMEM((1,), F32),
            pltpu.SMEM((1,), jnp.int32),
            pltpu.SMEM((1,), F32),
            vm((2, 4, HK, BK, D), BF16),
            vm((2, 4, HK, BK, D), BF16),
            vm((2, 2, 4, HK, BK, D), BF16),
            vm((2, 2, 4, HK, BK, D), BF16),
            vm((2, 4, HK, BK, D), F32),
            vm((3, HK, 2, BK, D), BF16),
            vm((3, HK, 2, BK, D), BF16),
            vm((2, 4, HK, BK, D), F32),
            vm((HK, NJ, JR, D), BF16),
            vm((2, rows, HK * D), BF16),
            vm((2, BK, HK * D), BF16),
            dma((17,)),
            dma((21,)),
            dma((HK, 2, 3)),
            dma((HK, 2, 3)),
            dma((HK, 4, 4)),
            dma((HK, 4, 4)),
            dma((max(mpn - 1, 1),)),
            dma((max(mpn - 1, 1),)),
            dma((2, 4, HK)),
            dma((2, 4, HK)),
            dma((2, 2, 4, HK)),
            dma((2, 2, 4, HK)),
            dma((3, HK)),
            dma((3, HK)),
        ],
        compiler_params=pltpu.CompilerParams(
            collective_id=0, has_side_effects=True, vmem_limit_bytes=63 * 1024 * 1024
        ),
        name="attention_gradient",
    )(q, rk, rv, pk, pv, ro, prox.reshape(1, rows), beh.reshape(1, rows), adv, lens,
      mask.reshape(1, rows))
    return pl.pallas_call(
        hand_over,
        out_shape=tuple(jax.ShapeDtypeStruct(o.shape, o.dtype) for o in outs),
        in_specs=[any_spec] * 6,
        out_specs=(any_spec,) * 6,
        scratch_shapes=[vm(o.shape, o.dtype) for o in outs[:5]]
        + [pltpu.SMEM((1,), F32), dma((2, 6))],
        compiler_params=pltpu.CompilerParams(vmem_limit_bytes=63 * 1024 * 1024),
        name="hand_over",
    )(*outs)


def solution(mesh):
    wide = P("dp", "mp")
    row = P("dp")
    return jax.shard_map(
        per_device,
        mesh=mesh,
        in_specs=(wide,) * 6 + (row,) * 5,
        out_specs=(wide,) * 5 + (row,),
        check_vma=False,
    )
```

```python
import functools
import math

import jax
import jax.numpy as jnp
from jax import lax
from jax.experimental import pallas as pl
from jax.experimental.pallas import tpu as pltpu
from jax.sharding import PartitionSpec as P

D = 128
HK = 2
NJ = 4
JR = 256
CK = 256
BK = 64
SCALE = 1.0 / math.sqrt(D)
C1 = SCALE * math.log2(math.e)
CLIP = 0.2
MESH = pl.DeviceIdType.MESH
F32 = jnp.float32
BF16 = jnp.bfloat16

OWN, UP, DOWN, FAR = 0, 1, 2, 3
RESP = 4 * CK
KEYS = RESP + 128
CHUNKS = [(0, CK), (CK, CK), (2 * CK, CK), (3 * CK, CK), (RESP, 128)]


def dot_t(a, b):
    return lax.dot_general(a, b, (((1,), (1,)), ((), ())), preferred_element_type=F32)


def dot_n(a, b):
    return jnp.dot(a, b, preferred_element_type=F32)


def kernel(
    q_hbm, rk_hbm, rv_hbm, pk_hbm, pv_hbm, ro_hbm, prox_hbm, beh_hbm, adv_hbm, len_hbm, mask_hbm,
    gq_out, grk_out, grv_out, gpk_out, gpv_out, loss_hbm,
    kv, kvt, qs, rs, rst, es, att, pb, ds, ms, ls, fs, hds, do,
    lpx, tok, tokm, adv_s, len_s, loss_s,
    y2s, y2r, y1s, y1r, joins, zs, zr, ownz,
    ld_sem, out_sem,
    gz_s, gz_r, gy_s, gy_r, lp_s, lp_r, y2_s, y2_rs, y1_s, y1_rs, z_s, z_rs,
):
    dp = lax.axis_index("dp")
    mp = lax.axis_index("mp")
    pc = lax.axis_size("dp") // 16
    mpn = lax.axis_size("mp")
    s = lax.rem(dp, pc)
    gp = dp // pc
    y = gp // 4
    z = lax.rem(gp, 4)

    def peer(dy, dz):
        yy = lax.rem(y + dy + 4, 4)
        zz = lax.rem(z + dz + 4, 4)
        return (((yy * 4 + zz) * pc + s), mp)

    y_up, y_dn, y_far = peer(1, 0), peer(-1, 0), peer(2, 0)
    z_up, z_dn, z_far = peer(0, 1), peer(0, -1), peer(0, 2)
    mates = [(dp, lax.rem(mp + k, mpn)) for k in range(1, mpn)]

    barrier = pltpu.get_barrier_semaphore()
    friends = [y_up, y_dn, y_far, z_up, z_dn] + mates
    for f in friends:
        pl.semaphore_signal(barrier, inc=1, device_id=f, device_id_type=MESH)

    own_loads = []
    for t, src in enumerate((pk_hbm, pv_hbm)):
        for h in range(HK):
            c = pltpu.make_async_copy(
                src.at[:, h * D:(h + 1) * D], kv.at[t, h, 0:BK, :], ld_sem.at[t * HK + h]
            )
            c.start()
            own_loads.append(c)
    resp_loads = []
    for t, src in enumerate((rk_hbm, rv_hbm)):
        for h in range(HK):
            c = pltpu.make_async_copy(
                src.at[:, h * D:(h + 1) * D], kv.at[t, h, RESP:KEYS, :], ld_sem.at[4 + t * HK + h]
            )
            c.start()
            resp_loads.append(c)
    for h in range(HK):
        for t, (src, dst) in enumerate(((q_hbm, qs), (ro_hbm, rs))):
            for i in range(8):
                n = h * 8 + i
                pltpu.make_async_copy(
                    src.at[:, n * D:(n + 1) * D],
                    dst.at[h, i // 2, (i % 2) * 128:(i % 2 + 1) * 128, :],
                    ld_sem.at[8 + t * HK + h],
                ).start()
    small = [
        pltpu.make_async_copy(prox_hbm, tok.at[0], ld_sem.at[12]),
        pltpu.make_async_copy(beh_hbm, tok.at[1], ld_sem.at[13]),
        pltpu.make_async_copy(mask_hbm, tokm, ld_sem.at[14]),
        pltpu.make_async_copy(adv_hbm, adv_s, ld_sem.at[15]),
        pltpu.make_async_copy(len_hbm, len_s, ld_sem.at[16]),
    ]
    for c in small:
        c.start()

    def wait_rows(h):
        for t, dst in enumerate((qs, rs)):
            pltpu.make_async_copy(dst.at[h], dst.at[h], ld_sem.at[8 + t * HK + h]).wait()

    def turn_rows(h):
        for j in range(NJ):
            rst[h, j] = rs[h, j].T

    sends = []

    def send(src, dst, ss, rsem, to):
        c = pltpu.make_async_remote_copy(
            src_ref=src, dst_ref=dst, send_sem=ss, recv_sem=rsem, device_id=to, device_id_type=MESH
        )
        c.start()
        sends.append(c)

    def arrived(dst, rsem):
        pltpu.make_async_remote_copy(
            src_ref=dst, dst_ref=dst, send_sem=rsem, recv_sem=rsem, device_id=y_up, device_id_type=MESH
        ).wait_recv()

    def kvb(t, h, dz, dy):
        lo = dz * CK + dy * BK
        return kv.at[t, h, lo:lo + BK, :]

    def move(t, h, a, b, ss, rsem, to):
        send(kvb(t, h, *a), kvb(t, h, *b), ss, rsem, to)

    def z_piece(t, h, way):
        move(t, h, (OWN, OWN), ((DOWN, UP)[way], OWN),
             gz_s.at[t, h, way], gz_r.at[t, h, way], (z_up, z_dn)[way])

    def z_pass(t, h):
        dz, n, to = (UP, 1, z_dn) if t == 0 else (DOWN, 0, z_up)
        arrived(kvb(t, h, dz, OWN), gz_r.at[t, h, n])
        move(t, h, (dz, OWN), (FAR, OWN), gz_s.at[t, h, 2], gz_r.at[t, h, 2], to)
        y_send(t, h, dz)

    def z_other(t, h):
        dz, n = (DOWN, 0) if t == 0 else (UP, 1)
        arrived(kvb(t, h, dz, OWN), gz_r.at[t, h, n])
        y_send(t, h, dz)

    def z_last(t, h):
        arrived(kvb(t, h, FAR, OWN), gz_r.at[t, h, 2])
        y_send(t, h, FAR)

    def y_send(t, h, dz):
        if dz in (OWN, FAR):
            move(t, h, (dz, OWN), (dz, FAR), gy_s.at[t, h, dz, 2], gy_r.at[t, h, dz, 2], y_far)
        move(t, h, (dz, OWN), (dz, DOWN), gy_s.at[t, h, dz, 0], gy_r.at[t, h, dz, 0], y_up)
        move(t, h, (dz, OWN), (dz, UP), gy_s.at[t, h, dz, 1], gy_r.at[t, h, dz, 1], y_dn)

    def z_fill(t, h):
        arrived(kvb(t, h, OWN, FAR), gy_r.at[t, h, OWN, 2])
        move(t, h, (OWN, FAR), (DOWN, FAR), gz_s.at[t, h, 3], gz_r.at[t, h, 3], z_up)
        move(t, h, (OWN, FAR), (UP, FAR), gz_s.at[t, h, 4], gz_r.at[t, h, 4], z_dn)

    def y_last(t, h, dz):
        arrived(kvb(t, h, dz, DOWN), gy_r.at[t, h, dz, 0])
        arrived(kvb(t, h, dz, UP), gy_r.at[t, h, dz, 1])
        if dz == FAR:
            arrived(kvb(t, h, dz, FAR), gy_r.at[t, h, dz, 2])
        elif dz != OWN:
            n = 3 if dz == DOWN else 4
            arrived(kvb(t, h, dz, FAR), gz_r.at[t, h, n])

    def fwd(h, ci):
        off, nk = CHUNKS[ci]

        def body(j, _):
            sc = dot_t(kv[0, h, off:off + nk, :], qs[h, j])
            if ci == 4:
                key = lax.broadcasted_iota(jnp.int32, (nk, JR), 0)
                row = lax.broadcasted_iota(jnp.int32, (nk, JR), 1)
                sc = jnp.where(key <= lax.rem(row, 128), sc, -jnp.inf)
            m = jnp.max(sc, axis=0, keepdims=True) * C1
            e = jnp.exp2(sc * C1 - m)
            es[h, j, off:off + nk, :] = e
            ms[h, j, ci:ci + 1, :] = m
            ls[h, j, ci:ci + 1, :] = jnp.sum(e, axis=0, keepdims=True)
            return 0

        lax.fori_loop(0, NJ, body, 0, unroll=True)

    def turn_keys(t, h, ci):
        off, nk = CHUNKS[ci]
        kvt[t, h, :, off:off + nk] = kv[t, h, off:off + nk, :].T

    def normalise(h):
        for j in range(NJ):
            mc = ms[h, j, 0:5, :]
            m = jnp.max(mc, axis=0, keepdims=True)
            f = jnp.exp2(mc - m)
            total = jnp.sum(f * ls[h, j, 0:5, :], axis=0, keepdims=True)
            f = f / total
            fs[h, j, 0:5, :] = f
            for ci, (off, nk) in enumerate(CHUNKS):
                pb[h, j, off:off + nk, :] = (
                    es[h, j, off:off + nk, :] * f[ci:ci + 1, :]
                ).astype(BF16)

    def attend(h):
        for dz in (OWN, UP, DOWN, 4):
            turn_keys(1, h, dz)
        for j in range(NJ):
            att[h, j] = dot_n(kvt[1, h, :, 0:3 * CK], pb[h, j, 0:3 * CK, :]) + dot_n(
                kvt[1, h, :, RESP:KEYS], pb[h, j, RESP:KEYS, :]
            )

    def attend_last(h, lp):
        turn_keys(1, h, FAR)
        for j in range(NJ):
            attended = att[h, j] + dot_n(kvt[1, h, :, 3 * CK:RESP], pb[h, j, 3 * CK:RESP, :])
            hd = jnp.sum(attended * rst[h, j].astype(F32), axis=0, keepdims=True)
            hds[h, j, 0:1, :] = hd
            lp = lp + hd[:, :128] + hd[:, 128:]
        return lp

    for c in own_loads:
        c.wait()
    pl.semaphore_wait(barrier, len(friends))
    heads = range(HK)
    for t in range(2):
        for h in heads:
            for way in range(2):
                z_piece(t if way else 1 - t, h, way)
    for t in range(2):
        for h in heads:
            y_send(t, h, OWN)
    for c in resp_loads:
        c.wait()
    wait_rows(0)
    fwd(0, 4)
    for h in heads:
        z_pass(0, h)
        z_pass(1, h)
    for t in range(2):
        for h in heads:
            z_other(t, h)
    for h in heads:
        z_fill(0, h)
    wait_rows(1)
    fwd(1, 4)
    for h in heads:
        z_last(0, h)
    for h in heads:
        z_fill(1, h)
    for h in heads:
        z_last(1, h)
    for h in heads:
        turn_rows(h)
        y_last(0, h, OWN)
        fwd(h, OWN)
    for h in heads:
        for dz in (UP, DOWN):
            y_last(0, h, dz)
            fwd(h, dz)
    for h in heads:
        y_last(0, h, FAR)
        fwd(h, FAR)
        normalise(h)
    for h in heads:
        for dz in (OWN, UP, DOWN):
            y_last(1, h, dz)
        attend(h)
    lp = jnp.zeros((1, 128), F32)
    for h in heads:
        y_last(1, h, FAR)
        lp = attend_last(h, lp)

    lpx[mp] = jnp.broadcast_to(lp, (8, 128))
    for k, mate in enumerate(mates):
        send(lpx.at[mp], lpx.at[mp], lp_s.at[k], lp_r.at[k], mate)
    for c in small:
        c.wait()
    for k in range(mpn - 1):
        src = lax.rem(mp + mpn - 1 - k, mpn)
        arrived(lpx.at[src], lp_r.at[k])
    log_prob = jnp.zeros((1, 128), F32)
    for k in range(mpn):
        log_prob = log_prob + lpx[k, 0:1, :]
    prox = tok[0]
    adv = adv_s[0]
    length = len_s[0]
    ratio = jnp.exp(log_prob - prox)
    importance = jnp.exp(prox - tok[1])
    squashed = jnp.tanh((ratio - 1.0) / CLIP)
    clipped = 1.0 + CLIP * squashed
    token = lax.broadcasted_iota(jnp.int32, (1, 128), 1)
    valid = (token < length) & (tokm[...] == 1)
    lens = jnp.broadcast_to(length, (1, 128)).astype(F32)
    token_scale = jnp.where(valid, 128.0 / lens, 0.0)
    slope = jnp.where(adv * (ratio - 1.0) > 0, 1.0 - squashed * squashed, 1.0)
    g = -token_scale * importance * adv * ratio * slope
    g_rows = jnp.concatenate([g, g], axis=1)
    g_cols = jnp.broadcast_to(g, (128, 128)).T
    g_cols = jnp.concatenate([g_cols, g_cols], axis=0)

    def grad_out(h):
        def body(j, _):
            do[h, j] = (g_cols * rs[h, j].astype(F32)).astype(BF16)
            return 0

        lax.fori_loop(0, NJ, body, 0, unroll=True)

    def value_grad(h, ci):
        off, nk = CHUNKS[ci]
        acc = dot_n(pb[h, 0, off:off + nk, :], do[h, 0])
        for j in range(1, NJ):
            acc = acc + dot_n(pb[h, j, off:off + nk, :], do[h, j])
        return acc

    def key_grad(h, ci):
        off, nk = CHUNKS[ci]
        acc = None
        for j in range(NJ):
            grad_probs = dot_t(kv[1, h, off:off + nk, :], do[h, j])
            d = (es[h, j, off:off + nk, :] * fs[h, j, ci:ci + 1, :]) * (
                grad_probs - hds[h, j, 0:1, :] * g_rows
            )
            d = d.astype(BF16)
            ds[h, j, off:off + nk, :] = d
            part = dot_n(d, qs[h, j])
            acc = part if acc is None else acc + part
        return acc * SCALE

    def rows_of(dy):
        return slice(dy * BK, (dy + 1) * BK)

    def terms(dz, h):
        v = value_grad(h, dz)
        y2s[0, dz, h] = v[rows_of(FAR)].astype(BF16)
        y1s[1, 0, dz, h] = v[rows_of(DOWN)].astype(BF16)
        first_sends(0, dz, h)
        joins[0, dz, h] = v[rows_of(UP)]
        ownz[0, dz, h] = v[rows_of(OWN)]
        k = key_grad(h, dz)
        y2s[1, dz, h] = k[rows_of(FAR)].astype(BF16)
        y1s[0, 1, dz, h] = k[rows_of(UP)].astype(BF16)
        first_sends(1, dz, h)
        joins[1, dz, h] = k[rows_of(DOWN)]
        ownz[1, dz, h] = k[rows_of(OWN)]

    def y1_send(way, t, dz, h):
        send(y1s.at[way, t, dz, h], y1r.at[way, t, dz, h],
             y1_s.at[way, t, dz, h], y1_rs.at[way, t, dz, h], y_up if way == 0 else y_dn)

    def first_sends(t, dz, h):
        send(y2s.at[t, dz, h], y2r.at[t, dz, h],
             y2_s.at[t, dz, h], y2_rs.at[t, dz, h], (y_up, y_dn)[t])
        y1_send(1 - t, t, dz, h)

    def join_sends(dz, h):
        for t in range(2):
            arrived(y2r.at[t, dz, h], y2_rs.at[t, dz, h])
            y1s[t, t, dz, h] = (joins[t, dz, h] + y2r[t, dz, h].astype(F32)).astype(BF16)
            y1_send(t, t, dz, h)

    def y_total(dz, h):
        for t in range(2):
            for way in range(2):
                arrived(y1r.at[way, t, dz, h], y1_rs.at[way, t, dz, h])
            total = ownz[t, dz, h] + (
                y1r[0, t, dz, h].astype(F32) + y1r[1, t, dz, h].astype(F32)
            )
            if dz == OWN:
                ownz[t, dz, h] = total
            else:
                zs[dz - 1, h, t] = total.astype(BF16)
        if dz != OWN:
            send(zs.at[dz - 1, h], zr.at[dz - 1, h], z_s.at[dz - 1, h], z_rs.at[dz - 1, h],
                 (z_up, z_dn, z_far)[dz - 1])

    GROUPS = ((FAR, 0), (FAR, 1), (UP, 0), (DOWN, 0), (UP, 1), (DOWN, 1), (OWN, 0), (OWN, 1))
    for n, group in enumerate(GROUPS):
        if n < HK:
            grad_out(n)
        terms(*group)
        if n >= 2:
            join_sends(*GROUPS[n - 2])
        if n >= 4:
            y_total(*GROUPS[n - 4])

    for n in (6, 7):
        join_sends(*GROUPS[n])
    y_total(*GROUPS[4])
    for h in range(HK):
        grk_out[:, h * D:(h + 1) * D] = key_grad(h, 4).astype(BF16)
        grv_out[:, h * D:(h + 1) * D] = value_grad(h, 4).astype(BF16)

    def query_grad(h):
        for j in range(NJ):
            d = (dot_n(kvt[0, h], ds[h, j]) * SCALE).T.astype(BF16)
            for i in range(2):
                n = h * 8 + j * 2 + i
                gq_out[:, n * D:(n + 1) * D] = d[i * 128:(i + 1) * 128]

    y_total(*GROUPS[5])
    for h in range(HK):
        for ci in range(5):
            turn_keys(0, h, ci)
        query_grad(h)
    objective = jnp.minimum(ratio * adv, clipped * adv)
    loss_s[0] = -jnp.sum(token_scale * importance * objective)
    loss_out = pltpu.make_async_copy(loss_s, loss_hbm, out_sem.at[0])
    loss_out.start()
    for h in range(HK):
        y_total(OWN, h)
    for h in range(HK):
        for b in (2, 0, 1):
            arrived(zr.at[b, h], z_rs.at[b, h])
        for t in range(2):
            total = ownz[t, OWN, h]
            for b in range(3):
                total = total + zr[b, h, t].astype(F32)
            (gpv_out, gpk_out)[t][:, h * D:(h + 1) * D] = total.astype(BF16)
    loss_out.wait()
    for c in sends:
        c.wait_send()


def hand_over(*refs):
    sem = refs[-1]
    copies = [pltpu.make_async_copy(refs[n], refs[6 + n], sem.at[n]) for n in range(6)]
    for c in copies:
        c.start()
    for c in copies:
        c.wait()


def per_device(q, rk, rv, pk, pv, ro, prox, beh, adv, lens, mask):
    rows = q.shape[0]
    any_spec = pl.BlockSpec(memory_space=pl.ANY)
    dma = pltpu.SemaphoreType.DMA
    vm = pltpu.VMEM
    mpn = lax.axis_size("mp")
    fixed = functools.partial(pltpu.with_memory_space_constraint, memory_space=pltpu.HBM)
    outs = pl.pallas_call(
        kernel,
        out_shape=(
            pltpu.VMEM(q.shape, BF16),
            pltpu.VMEM(rk.shape, BF16),
            pltpu.VMEM(rv.shape, BF16),
            pltpu.VMEM(pk.shape, BF16),
            pltpu.VMEM(pv.shape, BF16),
            jax.ShapeDtypeStruct((1,), F32),
        ),
        in_specs=[any_spec] * 11,
        out_specs=(pl.BlockSpec(memory_space=pltpu.VMEM),) * 5 + (any_spec,),
        scratch_shapes=[
            vm((2, HK, KEYS, D), BF16),
            vm((2, HK, D, KEYS), BF16),
            vm((HK, NJ, JR, D), BF16),
            vm((HK, NJ, JR, D), BF16),
            vm((HK, NJ, D, JR), BF16),
            vm((HK, NJ, KEYS, JR), F32),
            vm((HK, NJ, D, JR), F32),
            vm((HK, NJ, KEYS, JR), BF16),
            vm((HK, NJ, KEYS, JR), BF16),
            vm((HK, NJ, 8, JR), F32),
            vm((HK, NJ, 8, JR), F32),
            vm((HK, NJ, 8, JR), F32),
            vm((HK, NJ, 8, JR), F32),
            vm((HK, NJ, JR, D), BF16),
            vm((mpn, 8, 128), F32),
            vm((2, 1, 128), F32),
            vm((1, 128), jnp.int32),
            pltpu.SMEM((1,), F32),
            pltpu.SMEM((1,), jnp.int32),
            pltpu.SMEM((1,), F32),
            vm((2, 4, HK, BK, D), BF16),
            vm((2, 4, HK, BK, D), BF16),
            vm((2, 2, 4, HK, BK, D), BF16),
            vm((2, 2, 4, HK, BK, D), BF16),
            vm((2, 4, HK, BK, D), F32),
            vm((3, HK, 2, BK, D), BF16),
            vm((3, HK, 2, BK, D), BF16),
            vm((2, 4, HK, BK, D), F32),
            dma((17,)),
            dma((1,)),
            dma((2, HK, 5)),
            dma((2, HK, 5)),
            dma((2, HK, 4, 3)),
            dma((2, HK, 4, 3)),
            dma((max(mpn - 1, 1),)),
            dma((max(mpn - 1, 1),)),
            dma((2, 4, HK)),
            dma((2, 4, HK)),
            dma((2, 2, 4, HK)),
            dma((2, 2, 4, HK)),
            dma((3, HK)),
            dma((3, HK)),
        ],
        compiler_params=pltpu.CompilerParams(
            collective_id=0, has_side_effects=True, vmem_limit_bytes=48 * 1024 * 1024
        ),
        name="attention_gradient",
    )(*[fixed(a) for a in (q, rk, rv, pk, pv, ro, prox.reshape(1, rows), beh.reshape(1, rows))],
      adv, lens, fixed(mask.reshape(1, rows)))
    return pl.pallas_call(
        hand_over,
        out_shape=tuple(pltpu.HBM(o.shape, o.dtype) for o in outs),
        in_specs=[pl.BlockSpec(memory_space=pltpu.VMEM)] * 5 + [any_spec],
        out_specs=(any_spec,) * 6,
        scratch_shapes=[dma((6,))],
        name="hand_over",
    )(*[pltpu.with_memory_space_constraint(o, pltpu.VMEM) for o in outs[:5]], outs[5])


def solution(mesh):
    wide = P("dp", "mp")
    row = P("dp")
    return jax.shard_map(
        per_device,
        mesh=mesh,
        in_specs=(wide,) * 6 + (row,) * 5,
        out_specs=(wide,) * 5 + (row,),
        check_vma=False,
    )
```

```python
import functools
import math

import jax
import jax.numpy as jnp
from jax import lax
from jax.experimental import pallas as pl
from jax.experimental.pallas import tpu as pltpu
from jax.sharding import PartitionSpec as P

D = 128
HK = 2
NJ = 4
JR = 256
CK = 256
BK = 64
SCALE = 1.0 / math.sqrt(D)
C1 = SCALE * math.log2(math.e)
CLIP = 0.2
MESH = pl.DeviceIdType.MESH
F32 = jnp.float32
BF16 = jnp.bfloat16

OWN, UP, DOWN, FAR = 0, 1, 2, 3
RESP = 4 * CK
KEYS = RESP + 128
CHUNKS = [(0, CK), (CK, CK), (2 * CK, CK), (3 * CK, CK), (RESP, 128)]


def dot_t(a, b):
    return lax.dot_general(a, b, (((1,), (1,)), ((), ())), preferred_element_type=F32)


def dot_n(a, b):
    return jnp.dot(a, b, preferred_element_type=F32)


def kernel(
    q_hbm, rk_hbm, rv_hbm, pk_hbm, pv_hbm, ro_hbm, prox_hbm, beh_hbm, adv_hbm, len_hbm, mask_hbm,
    gq_out, grk_out, grv_out, gpk_out, gpv_out, loss_hbm,
    kv, kvt, qs, rs, rst, es, att, pb, ds, ms, ls, fs, hds, do,
    lpx, tok, tokm, adv_s, len_s, loss_s,
    y2s, y2r, y1s, y1r, joins, zs, zr, ownz,
    ld_sem, out_sem,
    gz_s, gz_r, gy_s, gy_r, lp_s, lp_r, y2_s, y2_rs, y1_s, y1_rs, z_s, z_rs,
):
    dp = lax.axis_index("dp")
    mp = lax.axis_index("mp")
    pc = lax.axis_size("dp") // 16
    mpn = lax.axis_size("mp")
    s = lax.rem(dp, pc)
    gp = dp // pc
    y = gp // 4
    z = lax.rem(gp, 4)

    def peer(dy, dz):
        yy = lax.rem(y + dy + 4, 4)
        zz = lax.rem(z + dz + 4, 4)
        return (((yy * 4 + zz) * pc + s), mp)

    y_up, y_dn, y_far = peer(1, 0), peer(-1, 0), peer(2, 0)
    z_up, z_dn, z_far = peer(0, 1), peer(0, -1), peer(0, 2)
    mates = [(dp, lax.rem(mp + k, mpn)) for k in range(1, mpn)]

    barrier = pltpu.get_barrier_semaphore()
    friends = [y_up, y_dn, y_far, z_up, z_dn] + mates
    for f in friends:
        pl.semaphore_signal(barrier, inc=1, device_id=f, device_id_type=MESH)

    own_loads = []
    for t, src in enumerate((pk_hbm, pv_hbm)):
        for h in range(HK):
            c = pltpu.make_async_copy(
                src.at[:, h * D:(h + 1) * D], kv.at[t, h, 0:BK, :], ld_sem.at[t * HK + h]
            )
            c.start()
            own_loads.append(c)
    resp_loads = []
    for t, src in enumerate((rk_hbm, rv_hbm)):
        for h in range(HK):
            c = pltpu.make_async_copy(
                src.at[:, h * D:(h + 1) * D], kv.at[t, h, RESP:KEYS, :], ld_sem.at[4 + t * HK + h]
            )
            c.start()
            resp_loads.append(c)
    for h in range(HK):
        for t, (src, dst) in enumerate(((q_hbm, qs), (ro_hbm, rs))):
            for i in range(8):
                n = h * 8 + i
                pltpu.make_async_copy(
                    src.at[:, n * D:(n + 1) * D],
                    dst.at[h, i // 2, (i % 2) * 128:(i % 2 + 1) * 128, :],
                    ld_sem.at[8 + t * HK + h],
                ).start()
    small = [
        pltpu.make_async_copy(prox_hbm, tok.at[0], ld_sem.at[12]),
        pltpu.make_async_copy(beh_hbm, tok.at[1], ld_sem.at[13]),
        pltpu.make_async_copy(mask_hbm, tokm, ld_sem.at[14]),
        pltpu.make_async_copy(adv_hbm, adv_s, ld_sem.at[15]),
        pltpu.make_async_copy(len_hbm, len_s, ld_sem.at[16]),
    ]
    for c in small:
        c.start()

    def wait_rows(h):
        for t, dst in enumerate((qs, rs)):
            pltpu.make_async_copy(dst.at[h], dst.at[h], ld_sem.at[8 + t * HK + h]).wait()

    def turn_rows(h):
        for j in range(NJ):
            rst[h, j] = rs[h, j].T

    sends = []

    def send(src, dst, ss, rsem, to):
        c = pltpu.make_async_remote_copy(
            src_ref=src, dst_ref=dst, send_sem=ss, recv_sem=rsem, device_id=to, device_id_type=MESH
        )
        c.start()
        sends.append(c)

    def settle():
        while sends:
            sends.pop(0).wait_send()

    def arrived(dst, rsem):
        pltpu.make_async_remote_copy(
            src_ref=dst, dst_ref=dst, send_sem=rsem, recv_sem=rsem, device_id=y_up, device_id_type=MESH
        ).wait_recv()

    def kvb(t, h, dz, dy):
        lo = dz * CK + dy * BK
        return kv.at[t, h, lo:lo + BK, :]

    def move(t, h, a, b, ss, rsem, to):
        send(kvb(t, h, *a), kvb(t, h, *b), ss, rsem, to)

    def z_piece(t, h, way):
        move(t, h, (OWN, OWN), ((DOWN, UP)[way], OWN),
             gz_s.at[t, h, way], gz_r.at[t, h, way], (z_up, z_dn)[way])

    def z_pass(t, h):
        dz, n, to = (UP, 1, z_dn) if t == 0 else (DOWN, 0, z_up)
        arrived(kvb(t, h, dz, OWN), gz_r.at[t, h, n])
        move(t, h, (dz, OWN), (FAR, OWN), gz_s.at[t, h, 2], gz_r.at[t, h, 2], to)
        y_send(t, h, dz)

    def z_other(t, h):
        dz, n = (DOWN, 0) if t == 0 else (UP, 1)
        arrived(kvb(t, h, dz, OWN), gz_r.at[t, h, n])
        y_send(t, h, dz)

    def z_last(t, h):
        arrived(kvb(t, h, FAR, OWN), gz_r.at[t, h, 2])
        y_send(t, h, FAR)

    def y_send(t, h, dz):
        if dz in (OWN, FAR):
            move(t, h, (dz, OWN), (dz, FAR), gy_s.at[t, h, dz, 2], gy_r.at[t, h, dz, 2], y_far)
        move(t, h, (dz, OWN), (dz, DOWN), gy_s.at[t, h, dz, 0], gy_r.at[t, h, dz, 0], y_up)
        move(t, h, (dz, OWN), (dz, UP), gy_s.at[t, h, dz, 1], gy_r.at[t, h, dz, 1], y_dn)

    def z_fill(t, h):
        arrived(kvb(t, h, OWN, FAR), gy_r.at[t, h, OWN, 2])
        move(t, h, (OWN, FAR), (DOWN, FAR), gz_s.at[t, h, 3], gz_r.at[t, h, 3], z_up)
        move(t, h, (OWN, FAR), (UP, FAR), gz_s.at[t, h, 4], gz_r.at[t, h, 4], z_dn)

    def y_last(t, h, dz):
        arrived(kvb(t, h, dz, DOWN), gy_r.at[t, h, dz, 0])
        arrived(kvb(t, h, dz, UP), gy_r.at[t, h, dz, 1])
        if dz == FAR:
            arrived(kvb(t, h, dz, FAR), gy_r.at[t, h, dz, 2])
        elif dz != OWN:
            n = 3 if dz == DOWN else 4
            arrived(kvb(t, h, dz, FAR), gz_r.at[t, h, n])

    def fwd(h, ci):
        off, nk = CHUNKS[ci]

        def body(j, _):
            sc = dot_t(kv[0, h, off:off + nk, :], qs[h, j])
            if ci == 4:
                key = lax.broadcasted_iota(jnp.int32, (nk, JR), 0)
                row = lax.broadcasted_iota(jnp.int32, (nk, JR), 1)
                sc = jnp.where(key <= lax.rem(row, 128), sc, -jnp.inf)
            m = jnp.max(sc, axis=0, keepdims=True) * C1
            e = jnp.exp2(sc * C1 - m)
            es[h, j, off:off + nk, :] = e
            ms[h, j, ci:ci + 1, :] = m
            ls[h, j, ci:ci + 1, :] = jnp.sum(e, axis=0, keepdims=True)
            return 0

        lax.fori_loop(0, NJ, body, 0, unroll=True)

    def turn_keys(t, h, ci):
        off, nk = CHUNKS[ci]
        kvt[t, h, :, off:off + nk] = kv[t, h, off:off + nk, :].T

    def normalise(h):
        for j in range(NJ):
            mc = ms[h, j, 0:5, :]
            m = jnp.max(mc, axis=0, keepdims=True)
            f = jnp.exp2(mc - m)
            total = jnp.sum(f * ls[h, j, 0:5, :], axis=0, keepdims=True)
            f = f / total
            fs[h, j, 0:5, :] = f
            for ci, (off, nk) in enumerate(CHUNKS):
                pb[h, j, off:off + nk, :] = (
                    es[h, j, off:off + nk, :] * f[ci:ci + 1, :]
                ).astype(BF16)

    def attend(h):
        for dz in (OWN, UP, DOWN, 4):
            turn_keys(1, h, dz)
        for j in range(NJ):
            att[h, j] = dot_n(kvt[1, h, :, 0:3 * CK], pb[h, j, 0:3 * CK, :]) + dot_n(
                kvt[1, h, :, RESP:KEYS], pb[h, j, RESP:KEYS, :]
            )

    def attend_last(h, lp):
        turn_keys(1, h, FAR)
        for j in range(NJ):
            attended = att[h, j] + dot_n(kvt[1, h, :, 3 * CK:RESP], pb[h, j, 3 * CK:RESP, :])
            hd = jnp.sum(attended * rst[h, j].astype(F32), axis=0, keepdims=True)
            hds[h, j, 0:1, :] = hd
            lp = lp + hd[:, :128] + hd[:, 128:]
        return lp

    for c in own_loads:
        c.wait()
    pl.semaphore_wait(barrier, len(friends))
    heads = range(HK)
    for t in range(2):
        for h in heads:
            for way in range(2):
                z_piece(t if way else 1 - t, h, way)
    for t in range(2):
        for h in heads:
            y_send(t, h, OWN)
    for c in resp_loads:
        c.wait()
    wait_rows(0)
    fwd(0, 4)
    for h in heads:
        z_pass(0, h)
        z_pass(1, h)
    for t in range(2):
        for h in heads:
            z_other(t, h)
    for h in heads:
        z_fill(0, h)
    wait_rows(1)
    fwd(1, 4)
    for h in heads:
        z_last(0, h)
    for h in heads:
        z_fill(1, h)
    for h in heads:
        z_last(1, h)
    for h in heads:
        turn_rows(h)
        y_last(0, h, OWN)
        fwd(h, OWN)
    for h in heads:
        for dz in (UP, DOWN):
            y_last(0, h, dz)
            fwd(h, dz)
    for h in heads:
        y_last(0, h, FAR)
        fwd(h, FAR)
        normalise(h)
    for h in heads:
        for dz in (OWN, UP, DOWN):
            y_last(1, h, dz)
        attend(h)
    lp = jnp.zeros((1, 128), F32)
    for h in heads:
        y_last(1, h, FAR)
        lp = attend_last(h, lp)

    lpx[mp] = jnp.broadcast_to(lp, (8, 128))
    for k, mate in enumerate(mates):
        send(lpx.at[mp], lpx.at[mp], lp_s.at[k], lp_r.at[k], mate)
    for c in small:
        c.wait()
    settle()
    for k in range(mpn - 1):
        src = lax.rem(mp + mpn - 1 - k, mpn)
        arrived(lpx.at[src], lp_r.at[k])
    log_prob = jnp.zeros((1, 128), F32)
    for k in range(mpn):
        log_prob = log_prob + lpx[k, 0:1, :]
    prox = tok[0]
    adv = adv_s[0]
    length = len_s[0]
    ratio = jnp.exp(log_prob - prox)
    importance = jnp.exp(prox - tok[1])
    squashed = jnp.tanh((ratio - 1.0) / CLIP)
    clipped = 1.0 + CLIP * squashed
    token = lax.broadcasted_iota(jnp.int32, (1, 128), 1)
    valid = (token < length) & (tokm[...] == 1)
    lens = jnp.broadcast_to(length, (1, 128)).astype(F32)
    token_scale = jnp.where(valid, 128.0 / lens, 0.0)
    slope = jnp.where(adv * (ratio - 1.0) > 0, 1.0 - squashed * squashed, 1.0)
    g = -token_scale * importance * adv * ratio * slope
    g_rows = jnp.concatenate([g, g], axis=1)
    g_cols = jnp.broadcast_to(g, (128, 128)).T
    g_cols = jnp.concatenate([g_cols, g_cols], axis=0)

    def grad_out(h):
        def body(j, _):
            do[h, j] = (g_cols * rs[h, j].astype(F32)).astype(BF16)
            return 0

        lax.fori_loop(0, NJ, body, 0, unroll=True)

    def value_grad(h, ci):
        off, nk = CHUNKS[ci]
        acc = dot_n(pb[h, 0, off:off + nk, :], do[h, 0])
        for j in range(1, NJ):
            acc = acc + dot_n(pb[h, j, off:off + nk, :], do[h, j])
        return acc

    def key_grad(h, ci):
        off, nk = CHUNKS[ci]
        acc = None
        for j in range(NJ):
            grad_probs = dot_t(kv[1, h, off:off + nk, :], do[h, j])
            d = (es[h, j, off:off + nk, :] * fs[h, j, ci:ci + 1, :]) * (
                grad_probs - hds[h, j, 0:1, :] * g_rows
            )
            d = d.astype(BF16)
            ds[h, j, off:off + nk, :] = d
            part = dot_n(d, qs[h, j])
            acc = part if acc is None else acc + part
        return acc * SCALE

    def rows_of(dy):
        return slice(dy * BK, (dy + 1) * BK)

    def terms(dz, h):
        v = value_grad(h, dz)
        y2s[0, dz, h] = v[rows_of(FAR)].astype(BF16)
        y1s[1, 0, dz, h] = v[rows_of(DOWN)].astype(BF16)
        if dz in DIRECT:
            y1s[0, 0, dz, h] = v[rows_of(UP)].astype(BF16)
        else:
            joins[0, dz, h] = v[rows_of(UP)]
        first_sends(0, dz, h)
        ownz[0, dz, h] = v[rows_of(OWN)]
        k = key_grad(h, dz)
        y2s[1, dz, h] = k[rows_of(FAR)].astype(BF16)
        y1s[0, 1, dz, h] = k[rows_of(UP)].astype(BF16)
        if dz in DIRECT:
            y1s[1, 1, dz, h] = k[rows_of(DOWN)].astype(BF16)
        else:
            joins[1, dz, h] = k[rows_of(DOWN)]
        first_sends(1, dz, h)
        ownz[1, dz, h] = k[rows_of(OWN)]

    def y1_send(way, t, dz, h):
        send(y1s.at[way, t, dz, h], y1r.at[way, t, dz, h],
             y1_s.at[way, t, dz, h], y1_rs.at[way, t, dz, h], y_up if way == 0 else y_dn)

    def first_sends(t, dz, h):
        straight = dz in DIRECT
        send(y2s.at[t, dz, h], y2r.at[t, dz, h],
             y2_s.at[t, dz, h], y2_rs.at[t, dz, h], y_far if straight else (y_up, y_dn)[t])
        y1_send(1 - t, t, dz, h)
        if straight:
            y1_send(t, t, dz, h)

    def join_sends(dz, h):
        if dz in DIRECT:
            return
        for t in range(2):
            arrived(y2r.at[t, dz, h], y2_rs.at[t, dz, h])
            y1s[t, t, dz, h] = (joins[t, dz, h] + y2r[t, dz, h].astype(F32)).astype(BF16)
            y1_send(t, t, dz, h)

    def y_total(dz, h):
        for t in range(2):
            for way in range(2):
                arrived(y1r.at[way, t, dz, h], y1_rs.at[way, t, dz, h])
            total = ownz[t, dz, h] + (
                y1r[0, t, dz, h].astype(F32) + y1r[1, t, dz, h].astype(F32)
            )
            if dz in DIRECT:
                arrived(y2r.at[t, dz, h], y2_rs.at[t, dz, h])
                total = total + y2r[t, dz, h].astype(F32)
            if dz == OWN:
                ownz[t, dz, h] = total
            else:
                zs[dz - 1, h, t] = total.astype(BF16)
        if dz != OWN:
            send(zs.at[dz - 1, h], zr.at[dz - 1, h], z_s.at[dz - 1, h], z_rs.at[dz - 1, h],
                 (z_up, z_dn, z_far)[dz - 1])

    DIRECT = (FAR,)
    GROUPS = ((FAR, 0), (FAR, 1), (UP, 0), (DOWN, 0), (UP, 1), (DOWN, 1), (OWN, 0), (OWN, 1))
    for n, group in enumerate(GROUPS):
        if n < HK:
            grad_out(n)
        terms(*group)
        if n >= 2:
            join_sends(*GROUPS[n - 2])
        if n >= 5:
            y_total(*GROUPS[n - 5])

    for n in (6, 7):
        join_sends(*GROUPS[n])
    y_total(*GROUPS[3])
    y_total(*GROUPS[4])
    for h in range(HK):
        grk_out[:, h * D:(h + 1) * D] = key_grad(h, 4).astype(BF16)
        grv_out[:, h * D:(h + 1) * D] = value_grad(h, 4).astype(BF16)

    def query_grad(h):
        for j in range(NJ):
            d = (dot_n(kvt[0, h], ds[h, j]) * SCALE).T.astype(BF16)
            for i in range(2):
                n = h * 8 + j * 2 + i
                gq_out[:, n * D:(n + 1) * D] = d[i * 128:(i + 1) * 128]

    y_total(*GROUPS[5])
    for h in range(HK):
        for ci in range(5):
            turn_keys(0, h, ci)
        query_grad(h)
    objective = jnp.minimum(ratio * adv, clipped * adv)
    loss_s[0] = -jnp.sum(token_scale * importance * objective)
    loss_out = pltpu.make_async_copy(loss_s, loss_hbm, out_sem.at[0])
    loss_out.start()
    for h in range(HK):
        y_total(OWN, h)
    settle()
    for h in range(HK):
        for b in (2, 0, 1):
            arrived(zr.at[b, h], z_rs.at[b, h])
        for t in range(2):
            total = ownz[t, OWN, h]
            for b in range(3):
                total = total + zr[b, h, t].astype(F32)
            (gpv_out, gpk_out)[t][:, h * D:(h + 1) * D] = total.astype(BF16)
    loss_out.wait()
    settle()


def hand_over(*refs):
    sem = refs[-1]
    copies = [pltpu.make_async_copy(refs[n], refs[6 + n], sem.at[n]) for n in range(6)]
    for c in copies:
        c.start()
    for c in copies:
        c.wait()


def per_device(q, rk, rv, pk, pv, ro, prox, beh, adv, lens, mask):
    rows = q.shape[0]
    any_spec = pl.BlockSpec(memory_space=pl.ANY)
    dma = pltpu.SemaphoreType.DMA
    vm = pltpu.VMEM
    mpn = lax.axis_size("mp")
    fixed = functools.partial(pltpu.with_memory_space_constraint, memory_space=pltpu.HBM)
    outs = pl.pallas_call(
        kernel,
        out_shape=(
            pltpu.VMEM(q.shape, BF16),
            pltpu.VMEM(rk.shape, BF16),
            pltpu.VMEM(rv.shape, BF16),
            pltpu.VMEM(pk.shape, BF16),
            pltpu.VMEM(pv.shape, BF16),
            jax.ShapeDtypeStruct((1,), F32),
        ),
        in_specs=[any_spec] * 11,
        out_specs=(pl.BlockSpec(memory_space=pltpu.VMEM),) * 5 + (any_spec,),
        scratch_shapes=[
            vm((2, HK, KEYS, D), BF16),
            vm((2, HK, D, KEYS), BF16),
            vm((HK, NJ, JR, D), BF16),
            vm((HK, NJ, JR, D), BF16),
            vm((HK, NJ, D, JR), BF16),
            vm((HK, NJ, KEYS, JR), F32),
            vm((HK, NJ, D, JR), F32),
            vm((HK, NJ, KEYS, JR), BF16),
            vm((HK, NJ, KEYS, JR), BF16),
            vm((HK, NJ, 8, JR), F32),
            vm((HK, NJ, 8, JR), F32),
            vm((HK, NJ, 8, JR), F32),
            vm((HK, NJ, 8, JR), F32),
            vm((HK, NJ, JR, D), BF16),
            vm((mpn, 8, 128), F32),
            vm((2, 1, 128), F32),
            vm((1, 128), jnp.int32),
            pltpu.SMEM((1,), F32),
            pltpu.SMEM((1,), jnp.int32),
            pltpu.SMEM((1,), F32),
            vm((2, 4, HK, BK, D), BF16),
            vm((2, 4, HK, BK, D), BF16),
            vm((2, 2, 4, HK, BK, D), BF16),
            vm((2, 2, 4, HK, BK, D), BF16),
            vm((2, 4, HK, BK, D), F32),
            vm((3, HK, 2, BK, D), BF16),
            vm((3, HK, 2, BK, D), BF16),
            vm((2, 4, HK, BK, D), F32),
            dma((17,)),
            dma((1,)),
            dma((2, HK, 5)),
            dma((2, HK, 5)),
            dma((2, HK, 4, 3)),
            dma((2, HK, 4, 3)),
            dma((max(mpn - 1, 1),)),
            dma((max(mpn - 1, 1),)),
            dma((2, 4, HK)),
            dma((2, 4, HK)),
            dma((2, 2, 4, HK)),
            dma((2, 2, 4, HK)),
            dma((3, HK)),
            dma((3, HK)),
        ],
        compiler_params=pltpu.CompilerParams(
            collective_id=0, has_side_effects=True, vmem_limit_bytes=48 * 1024 * 1024
        ),
        name="attention_gradient",
    )(*[fixed(a) for a in (q, rk, rv, pk, pv, ro, prox.reshape(1, rows), beh.reshape(1, rows))],
      adv, lens, fixed(mask.reshape(1, rows)))
    return pl.pallas_call(
        hand_over,
        out_shape=tuple(pltpu.HBM(o.shape, o.dtype) for o in outs),
        in_specs=[pl.BlockSpec(memory_space=pltpu.VMEM)] * 5 + [any_spec],
        out_specs=(any_spec,) * 6,
        scratch_shapes=[dma((6,))],
        name="hand_over",
    )(*[pltpu.with_memory_space_constraint(o, pltpu.VMEM) for o in outs[:5]], outs[5])


def solution(mesh):
    wide = P("dp", "mp")
    row = P("dp")
    return jax.shard_map(
        per_device,
        mesh=mesh,
        in_specs=(wide,) * 6 + (row,) * 5,
        out_specs=(wide,) * 5 + (row,),
        check_vma=False,
    )
```

```python
import functools
import math

import jax
import jax.numpy as jnp
from jax import lax
from jax.experimental import pallas as pl
from jax.experimental.pallas import tpu as pltpu
from jax.sharding import PartitionSpec as P

D = 128
HK = 2
NJ = 4
JR = 256
CK = 256
BK = 64
SCALE = 1.0 / math.sqrt(D)
C1 = SCALE * math.log2(math.e)
CLIP = 0.2
MESH = pl.DeviceIdType.MESH
F32 = jnp.float32
BF16 = jnp.bfloat16

OWN, UP, DOWN, FAR = 0, 1, 2, 3
RESP = 4 * CK
KEYS = RESP + 128
CHUNKS = [(0, CK), (CK, CK), (2 * CK, CK), (3 * CK, CK), (RESP, 128)]


def dot_t(a, b):
    return lax.dot_general(a, b, (((1,), (1,)), ((), ())), preferred_element_type=F32)


def dot_n(a, b):
    return jnp.dot(a, b, preferred_element_type=F32)


def kernel(
    q_hbm, rk_hbm, rv_hbm, pk_hbm, pv_hbm, ro_hbm, prox_hbm, beh_hbm, adv_hbm, len_hbm, mask_hbm,
    gq_out, grk_out, grv_out, gpk_out, gpv_out, loss_out,
    kv, kvt, qs, rs, rst, es, att, pb, ds, ms, ls, fs, hds, do,
    lpx, tok, tokm, adv_s, len_s, loss_s,
    y2s, y2r, y1s, y1r, joins, zs, zr, ownz,
    ld_sem, out_sem,
    gz_s, gz_r, gy_s, gy_r, lp_s, lp_r, y2_s, y2_rs, y1_s, y1_rs, z_s, z_rs,
):
    dp = lax.axis_index("dp")
    mp = lax.axis_index("mp")
    pc = lax.axis_size("dp") // 16
    mpn = lax.axis_size("mp")
    s = lax.rem(dp, pc)
    gp = dp // pc
    y = gp // 4
    z = lax.rem(gp, 4)

    def peer(dy, dz):
        yy = lax.rem(y + dy + 4, 4)
        zz = lax.rem(z + dz + 4, 4)
        return (((yy * 4 + zz) * pc + s), mp)

    y_up, y_dn, y_far = peer(1, 0), peer(-1, 0), peer(2, 0)
    z_up, z_dn, z_far = peer(0, 1), peer(0, -1), peer(0, 2)
    mates = [(dp, lax.rem(mp + k, mpn)) for k in range(1, mpn)]

    barrier = pltpu.get_barrier_semaphore()
    friends = [y_up, y_dn, y_far, z_up, z_dn] + mates
    for f in friends:
        pl.semaphore_signal(barrier, inc=1, device_id=f, device_id_type=MESH)

    own_loads = []
    for t, src in enumerate((pk_hbm, pv_hbm)):
        for h in range(HK):
            c = pltpu.make_async_copy(
                src.at[:, h * D:(h + 1) * D], kv.at[t, h, 0:BK, :], ld_sem.at[t * HK + h]
            )
            c.start()
            own_loads.append(c)
    resp_loads = []
    for t, src in enumerate((rk_hbm, rv_hbm)):
        for h in range(HK):
            c = pltpu.make_async_copy(
                src.at[:, h * D:(h + 1) * D], kv.at[t, h, RESP:KEYS, :], ld_sem.at[4 + t * HK + h]
            )
            c.start()
            resp_loads.append(c)
    for h in range(HK):
        for t, (src, dst) in enumerate(((q_hbm, qs), (ro_hbm, rs))):
            for i in range(8):
                n = h * 8 + i
                pltpu.make_async_copy(
                    src.at[:, n * D:(n + 1) * D],
                    dst.at[h, i // 2, (i % 2) * 128:(i % 2 + 1) * 128, :],
                    ld_sem.at[8 + t * HK + h],
                ).start()
    small = [
        pltpu.make_async_copy(prox_hbm, tok.at[0], ld_sem.at[12]),
        pltpu.make_async_copy(beh_hbm, tok.at[1], ld_sem.at[13]),
        pltpu.make_async_copy(mask_hbm, tokm, ld_sem.at[14]),
        pltpu.make_async_copy(adv_hbm, adv_s, ld_sem.at[15]),
        pltpu.make_async_copy(len_hbm, len_s, ld_sem.at[16]),
    ]
    for c in small:
        c.start()

    def wait_rows(h):
        for t, dst in enumerate((qs, rs)):
            pltpu.make_async_copy(dst.at[h], dst.at[h], ld_sem.at[8 + t * HK + h]).wait()

    def turn_rows(h):
        for j in range(NJ):
            rst[h, j] = rs[h, j].T

    sends = []

    def send(src, dst, ss, rsem, to):
        c = pltpu.make_async_remote_copy(
            src_ref=src, dst_ref=dst, send_sem=ss, recv_sem=rsem, device_id=to, device_id_type=MESH
        )
        c.start()
        sends.append(c)

    def settle():
        while sends:
            sends.pop(0).wait_send()

    def arrived(dst, rsem):
        pltpu.make_async_remote_copy(
            src_ref=dst, dst_ref=dst, send_sem=rsem, recv_sem=rsem, device_id=y_up, device_id_type=MESH
        ).wait_recv()

    def kvb(t, h, dz, dy):
        lo = dz * CK + dy * BK
        return kv.at[t, h, lo:lo + BK, :]

    def move(t, h, a, b, ss, rsem, to):
        send(kvb(t, h, *a), kvb(t, h, *b), ss, rsem, to)

    def z_piece(t, h, way):
        move(t, h, (OWN, OWN), ((DOWN, UP)[way], OWN),
             gz_s.at[t, h, way], gz_r.at[t, h, way], (z_up, z_dn)[way])

    def z_pass(t, h):
        dz, n, to = (UP, 1, z_dn) if t == 0 else (DOWN, 0, z_up)
        arrived(kvb(t, h, dz, OWN), gz_r.at[t, h, n])
        move(t, h, (dz, OWN), (FAR, OWN), gz_s.at[t, h, 2], gz_r.at[t, h, 2], to)
        y_send(t, h, dz)

    def z_other(t, h):
        dz, n = (DOWN, 0) if t == 0 else (UP, 1)
        arrived(kvb(t, h, dz, OWN), gz_r.at[t, h, n])
        y_send(t, h, dz)

    def z_last(t, h):
        arrived(kvb(t, h, FAR, OWN), gz_r.at[t, h, 2])
        y_send(t, h, FAR)

    def y_send(t, h, dz):
        if dz in (OWN, FAR):
            move(t, h, (dz, OWN), (dz, FAR), gy_s.at[t, h, dz, 2], gy_r.at[t, h, dz, 2], y_far)
        move(t, h, (dz, OWN), (dz, DOWN), gy_s.at[t, h, dz, 0], gy_r.at[t, h, dz, 0], y_up)
        move(t, h, (dz, OWN), (dz, UP), gy_s.at[t, h, dz, 1], gy_r.at[t, h, dz, 1], y_dn)

    def z_fill(t, h):
        arrived(kvb(t, h, OWN, FAR), gy_r.at[t, h, OWN, 2])
        move(t, h, (OWN, FAR), (DOWN, FAR), gz_s.at[t, h, 3], gz_r.at[t, h, 3], z_up)
        move(t, h, (OWN, FAR), (UP, FAR), gz_s.at[t, h, 4], gz_r.at[t, h, 4], z_dn)

    def y_last(t, h, dz):
        arrived(kvb(t, h, dz, DOWN), gy_r.at[t, h, dz, 0])
        arrived(kvb(t, h, dz, UP), gy_r.at[t, h, dz, 1])
        if dz == FAR:
            arrived(kvb(t, h, dz, FAR), gy_r.at[t, h, dz, 2])
        elif dz != OWN:
            n = 3 if dz == DOWN else 4
            arrived(kvb(t, h, dz, FAR), gz_r.at[t, h, n])

    def fwd(h, ci):
        off, nk = CHUNKS[ci]

        def body(j, _):
            sc = dot_t(kv[0, h, off:off + nk, :], qs[h, j])
            if ci == 4:
                key = lax.broadcasted_iota(jnp.int32, (nk, JR), 0)
                row = lax.broadcasted_iota(jnp.int32, (nk, JR), 1)
                sc = jnp.where(key <= lax.rem(row, 128), sc, -jnp.inf)
            m = jnp.max(sc, axis=0, keepdims=True) * C1
            e = jnp.exp2(sc * C1 - m)
            es[h, j, off:off + nk, :] = e
            ms[h, j, ci:ci + 1, :] = m
            ls[h, j, ci:ci + 1, :] = jnp.sum(e, axis=0, keepdims=True)
            return 0

        lax.fori_loop(0, NJ, body, 0, unroll=True)

    def turn_keys(t, h, ci):
        off, nk = CHUNKS[ci]
        kvt[t, h, :, off:off + nk] = kv[t, h, off:off + nk, :].T

    def normalise(h):
        for j in range(NJ):
            mc = ms[h, j, 0:5, :]
            m = jnp.max(mc, axis=0, keepdims=True)
            f = jnp.exp2(mc - m)
            total = jnp.sum(f * ls[h, j, 0:5, :], axis=0, keepdims=True)
            f = f / total
            fs[h, j, 0:5, :] = f
            for ci, (off, nk) in enumerate(CHUNKS):
                pb[h, j, off:off + nk, :] = (
                    es[h, j, off:off + nk, :] * f[ci:ci + 1, :]
                ).astype(BF16)

    def attend(h):
        for dz in (OWN, UP, DOWN, 4):
            turn_keys(1, h, dz)
        for j in range(NJ):
            att[h, j] = dot_n(kvt[1, h, :, 0:3 * CK], pb[h, j, 0:3 * CK, :]) + dot_n(
                kvt[1, h, :, RESP:KEYS], pb[h, j, RESP:KEYS, :]
            )

    def attend_last(h, lp):
        turn_keys(1, h, FAR)
        for j in range(NJ):
            attended = att[h, j] + dot_n(kvt[1, h, :, 3 * CK:RESP], pb[h, j, 3 * CK:RESP, :])
            hd = jnp.sum(attended * rst[h, j].astype(F32), axis=0, keepdims=True)
            hds[h, j, 0:1, :] = hd
            lp = lp + hd[:, :128] + hd[:, 128:]
        return lp

    for c in own_loads:
        c.wait()
    pl.semaphore_wait(barrier, len(friends))
    heads = range(HK)
    for t in range(2):
        for h in heads:
            for way in range(2):
                z_piece(t if way else 1 - t, h, way)
    for t in range(2):
        for h in heads:
            y_send(t, h, OWN)
    for c in resp_loads:
        c.wait()
    wait_rows(0)
    fwd(0, 4)
    for h in heads:
        z_pass(0, h)
        z_pass(1, h)
    for t in range(2):
        for h in heads:
            z_other(t, h)
    for h in heads:
        z_fill(0, h)
    wait_rows(1)
    fwd(1, 4)
    for h in heads:
        z_last(0, h)
    for h in heads:
        z_fill(1, h)
    for h in heads:
        z_last(1, h)
    for h in heads:
        turn_rows(h)
        y_last(0, h, OWN)
        fwd(h, OWN)
    for h in heads:
        for dz in (UP, DOWN):
            y_last(0, h, dz)
            fwd(h, dz)
    for h in heads:
        y_last(0, h, FAR)
        fwd(h, FAR)
        normalise(h)
    for h in heads:
        for dz in (OWN, UP, DOWN):
            y_last(1, h, dz)
        attend(h)
    lp = jnp.zeros((1, 128), F32)
    for h in heads:
        y_last(1, h, FAR)
        lp = attend_last(h, lp)

    lpx[mp] = jnp.broadcast_to(lp, (8, 128))
    for k, mate in enumerate(mates):
        send(lpx.at[mp], lpx.at[mp], lp_s.at[k], lp_r.at[k], mate)
    for c in small:
        c.wait()
    settle()
    for k in range(mpn - 1):
        src = lax.rem(mp + mpn - 1 - k, mpn)
        arrived(lpx.at[src], lp_r.at[k])
    log_prob = jnp.zeros((1, 128), F32)
    for k in range(mpn):
        log_prob = log_prob + lpx[k, 0:1, :]
    prox = tok[0]
    adv = adv_s[0]
    length = len_s[0]
    ratio = jnp.exp(log_prob - prox)
    importance = jnp.exp(prox - tok[1])
    squashed = jnp.tanh((ratio - 1.0) / CLIP)
    clipped = 1.0 + CLIP * squashed
    token = lax.broadcasted_iota(jnp.int32, (1, 128), 1)
    valid = (token < length) & (tokm[...] == 1)
    lens = jnp.broadcast_to(length, (1, 128)).astype(F32)
    token_scale = jnp.where(valid, 128.0 / lens, 0.0)
    slope = jnp.where(adv * (ratio - 1.0) > 0, 1.0 - squashed * squashed, 1.0)
    g = -token_scale * importance * adv * ratio * slope
    g_rows = jnp.concatenate([g, g], axis=1)
    g_cols = jnp.broadcast_to(g, (128, 128)).T
    g_cols = jnp.concatenate([g_cols, g_cols], axis=0)

    def grad_out(h):
        def body(j, _):
            do[h, j] = (g_cols * rs[h, j].astype(F32)).astype(BF16)
            return 0

        lax.fori_loop(0, NJ, body, 0, unroll=True)

    def value_grad(h, ci):
        off, nk = CHUNKS[ci]
        acc = dot_n(pb[h, 0, off:off + nk, :], do[h, 0])
        for j in range(1, NJ):
            acc = acc + dot_n(pb[h, j, off:off + nk, :], do[h, j])
        return acc

    def key_grad(h, ci):
        off, nk = CHUNKS[ci]
        acc = None
        for j in range(NJ):
            grad_probs = dot_t(kv[1, h, off:off + nk, :], do[h, j])
            d = (es[h, j, off:off + nk, :] * fs[h, j, ci:ci + 1, :]) * (
                grad_probs - hds[h, j, 0:1, :] * g_rows
            )
            d = d.astype(BF16)
            ds[h, j, off:off + nk, :] = d
            part = dot_n(d, qs[h, j])
            acc = part if acc is None else acc + part
        return acc * SCALE

    def rows_of(dy):
        return slice(dy * BK, (dy + 1) * BK)

    def terms(dz, h):
        v = value_grad(h, dz)
        y2s[0, dz, h] = v[rows_of(FAR)].astype(BF16)
        y1s[1, 0, dz, h] = v[rows_of(DOWN)].astype(BF16)
        if dz in DIRECT:
            y1s[0, 0, dz, h] = v[rows_of(UP)].astype(BF16)
        else:
            joins[0, dz, h] = v[rows_of(UP)]
        first_sends(0, dz, h)
        ownz[0, dz, h] = v[rows_of(OWN)]
        k = key_grad(h, dz)
        y2s[1, dz, h] = k[rows_of(FAR)].astype(BF16)
        y1s[0, 1, dz, h] = k[rows_of(UP)].astype(BF16)
        if dz in DIRECT:
            y1s[1, 1, dz, h] = k[rows_of(DOWN)].astype(BF16)
        else:
            joins[1, dz, h] = k[rows_of(DOWN)]
        first_sends(1, dz, h)
        ownz[1, dz, h] = k[rows_of(OWN)]

    def y1_send(way, t, dz, h):
        send(y1s.at[way, t, dz, h], y1r.at[way, t, dz, h],
             y1_s.at[way, t, dz, h], y1_rs.at[way, t, dz, h], y_up if way == 0 else y_dn)

    def first_sends(t, dz, h):
        straight = dz in DIRECT
        send(y2s.at[t, dz, h], y2r.at[t, dz, h],
             y2_s.at[t, dz, h], y2_rs.at[t, dz, h], y_far if straight else (y_up, y_dn)[t])
        y1_send(1 - t, t, dz, h)
        if straight:
            y1_send(t, t, dz, h)

    def join_sends(dz, h):
        if dz in DIRECT:
            return
        for t in range(2):
            arrived(y2r.at[t, dz, h], y2_rs.at[t, dz, h])
            y1s[t, t, dz, h] = (joins[t, dz, h] + y2r[t, dz, h].astype(F32)).astype(BF16)
            y1_send(t, t, dz, h)

    def y_total(dz, h):
        for t in range(2):
            for way in range(2):
                arrived(y1r.at[way, t, dz, h], y1_rs.at[way, t, dz, h])
            total = ownz[t, dz, h] + (
                y1r[0, t, dz, h].astype(F32) + y1r[1, t, dz, h].astype(F32)
            )
            if dz in DIRECT:
                arrived(y2r.at[t, dz, h], y2_rs.at[t, dz, h])
                total = total + y2r[t, dz, h].astype(F32)
            if dz == OWN:
                ownz[t, dz, h] = total
            else:
                zs[dz - 1, h, t] = total.astype(BF16)
        if dz != OWN:
            send(zs.at[dz - 1, h], zr.at[dz - 1, h], z_s.at[dz - 1, h], z_rs.at[dz - 1, h],
                 (z_up, z_dn, z_far)[dz - 1])

    DIRECT = (FAR,)
    GROUPS = ((FAR, 0), (FAR, 1), (UP, 0), (DOWN, 0), (UP, 1), (DOWN, 1), (OWN, 0), (OWN, 1))
    for n, group in enumerate(GROUPS):
        if n < HK:
            grad_out(n)
        terms(*group)
        if n >= 2:
            join_sends(*GROUPS[n - 2])
        if n >= 5:
            y_total(*GROUPS[n - 5])

    for n in (6, 7):
        join_sends(*GROUPS[n])
    y_total(*GROUPS[3])
    y_total(*GROUPS[4])
    for h in range(HK):
        grk_out[:, h * D:(h + 1) * D] = key_grad(h, 4).astype(BF16)
        grv_out[:, h * D:(h + 1) * D] = value_grad(h, 4).astype(BF16)

    def query_grad(h):
        for j in range(NJ):
            d = (dot_n(kvt[0, h], ds[h, j]) * SCALE).T.astype(BF16)
            for i in range(2):
                n = h * 8 + j * 2 + i
                gq_out[:, n * D:(n + 1) * D] = d[i * 128:(i + 1) * 128]

    y_total(*GROUPS[5])
    for h in range(HK):
        for ci in range(5):
            turn_keys(0, h, ci)
        query_grad(h)
    objective = jnp.minimum(ratio * adv, clipped * adv)
    loss_out[0] = -jnp.sum(token_scale * importance * objective)
    for h in range(HK):
        y_total(OWN, h)
    settle()
    for h in range(HK):
        for b in (2, 0, 1):
            arrived(zr.at[b, h], z_rs.at[b, h])
        for t in range(2):
            total = ownz[t, OWN, h]
            for b in range(3):
                total = total + zr[b, h, t].astype(F32)
            (gpv_out, gpk_out)[t][:, h * D:(h + 1) * D] = total.astype(BF16)
    settle()


def hand_over(*refs):
    sem = refs[-1]
    copies = [pltpu.make_async_copy(refs[n], refs[6 + n], sem.at[n]) for n in range(6)]
    for c in copies:
        c.start()
    for c in copies:
        c.wait()


def per_device(q, rk, rv, pk, pv, ro, prox, beh, adv, lens, mask):
    rows = q.shape[0]
    any_spec = pl.BlockSpec(memory_space=pl.ANY)
    dma = pltpu.SemaphoreType.DMA
    vm = pltpu.VMEM
    mpn = lax.axis_size("mp")
    fixed = functools.partial(pltpu.with_memory_space_constraint, memory_space=pltpu.HBM)
    outs = pl.pallas_call(
        kernel,
        out_shape=(
            pltpu.VMEM(q.shape, BF16),
            pltpu.VMEM(rk.shape, BF16),
            pltpu.VMEM(rv.shape, BF16),
            pltpu.VMEM(pk.shape, BF16),
            pltpu.VMEM(pv.shape, BF16),
            pltpu.SMEM((1,), F32),
        ),
        in_specs=[any_spec] * 11,
        out_specs=(pl.BlockSpec(memory_space=pltpu.VMEM),) * 5
        + (pl.BlockSpec(memory_space=pltpu.SMEM),),
        scratch_shapes=[
            vm((2, HK, KEYS, D), BF16),
            vm((2, HK, D, KEYS), BF16),
            vm((HK, NJ, JR, D), BF16),
            vm((HK, NJ, JR, D), BF16),
            vm((HK, NJ, D, JR), BF16),
            vm((HK, NJ, KEYS, JR), F32),
            vm((HK, NJ, D, JR), F32),
            vm((HK, NJ, KEYS, JR), BF16),
            vm((HK, NJ, KEYS, JR), BF16),
            vm((HK, NJ, 8, JR), F32),
            vm((HK, NJ, 8, JR), F32),
            vm((HK, NJ, 8, JR), F32),
            vm((HK, NJ, 8, JR), F32),
            vm((HK, NJ, JR, D), BF16),
            vm((mpn, 8, 128), F32),
            vm((2, 1, 128), F32),
            vm((1, 128), jnp.int32),
            pltpu.SMEM((1,), F32),
            pltpu.SMEM((1,), jnp.int32),
            pltpu.SMEM((1,), F32),
            vm((2, 4, HK, BK, D), BF16),
            vm((2, 4, HK, BK, D), BF16),
            vm((2, 2, 4, HK, BK, D), BF16),
            vm((2, 2, 4, HK, BK, D), BF16),
            vm((2, 4, HK, BK, D), F32),
            vm((3, HK, 2, BK, D), BF16),
            vm((3, HK, 2, BK, D), BF16),
            vm((2, 4, HK, BK, D), F32),
            dma((17,)),
            dma((1,)),
            dma((2, HK, 5)),
            dma((2, HK, 5)),
            dma((2, HK, 4, 3)),
            dma((2, HK, 4, 3)),
            dma((max(mpn - 1, 1),)),
            dma((max(mpn - 1, 1),)),
            dma((2, 4, HK)),
            dma((2, 4, HK)),
            dma((2, 2, 4, HK)),
            dma((2, 2, 4, HK)),
            dma((3, HK)),
            dma((3, HK)),
        ],
        compiler_params=pltpu.CompilerParams(
            collective_id=0, has_side_effects=True, vmem_limit_bytes=48 * 1024 * 1024
        ),
        name="attention_gradient",
    )(*[fixed(a) for a in (q, rk, rv, pk, pv, ro, prox.reshape(1, rows), beh.reshape(1, rows))],
      adv, lens, fixed(mask.reshape(1, rows)))
    return pl.pallas_call(
        hand_over,
        out_shape=tuple(pltpu.HBM(o.shape, o.dtype) for o in outs),
        in_specs=[pl.BlockSpec(memory_space=pltpu.VMEM)] * 5 + [pl.BlockSpec(memory_space=pltpu.SMEM)],
        out_specs=(any_spec,) * 6,
        scratch_shapes=[dma((6,))],
        name="hand_over",
    )(*[pltpu.with_memory_space_constraint(o, pltpu.VMEM) for o in outs[:5]], outs[5])


def solution(mesh):
    wide = P("dp", "mp")
    row = P("dp")
    return jax.shard_map(
        per_device,
        mesh=mesh,
        in_specs=(wide,) * 6 + (row,) * 5,
        out_specs=(wide,) * 5 + (row,),
        check_vma=False,
    )
```
